512 devices in a mesh: tensor: 16 (over z_hi, y, core), context: 32 (over x, z_lo).
Axes of the slice: x: 4, y: 4, z: 16 (z_hi: 2, z_lo: 8; z = z_hi * 8 + z_lo), core: 2. Of those that a mesh axis runs over, the one named last changes fastest.
Arguments:
- gate_act: bfloat16 [16384, 4096], P('context', 'tensor'), may hold values from -6 to 6
- key_act: bfloat16 [16384, 4096], P('context', 'tensor'), may hold values from -6 to 6
- value_act: bfloat16 [16384, 4096], P('context', 'tensor'), may hold values from -6 to 6
- decay_rate: float32 [4096, 16], P('tensor'), may hold values from 3.0517578e-05 to 0.05
- residue: float32 [4096, 16], P('tensor'), may hold values from -1.5 to 1.5
- skip: float32 [4096], P('tensor'), may hold values from 0.5 to 1.5
- out_weight: bfloat16 [4096, 4096], P(None, 'tensor'), may hold values from -0.09375 to 0.09375
Outputs:
- layer_out: bfloat16 [16384, 4096], P('context', 'tensor')
The draws below stay inside these ranges and needn't reach their ends.
All inputs are finite; a program needn't handle non-finite values.
Results may differ from the reference program's by a relative error of at most 0.015.
Values may be sent and summed in bfloat16 or wider, within the bound.
No kernel may reach another device: no remote copies, remote signals or barrier semaphores. Data moves between devices by JAX's collectives and lax.ppermute only.
A program may use at most 64 MiB of HBM per device.

```python
import math
import jax
import jax.numpy as jnp
from jax import lax

D = 4096
MODES = 16
TOKENS = 16384


def level_of(rng, shape, cuts, smallest, top_value):
    level, own = 1.0, jax.random.fold_in(rng, 6)
    for dim, blocks in cuts:
        steps = jnp.exp(jax.random.uniform(jax.random.fold_in(own, dim), (blocks,), jnp.float32, smallest / len(cuts), top_value / len(cuts)))
        level = level * jnp.repeat(steps, shape[dim] // blocks).reshape([-1 if axis == dim else 1 for axis in range(len(shape))])
    return level


def gaussian(key, dims, scale, bound, split=(), held_as=jnp.bfloat16):
    drawn = jax.random.normal(key, dims, jnp.float32) * scale
    if len(split) > 0:
        drawn = level_of(key, dims, split, -0.22, 0.18) * drawn
    return jnp.clip(drawn, min=-bound, max=bound).astype(held_as)


def setup_inputs(seed: int = 0) -> dict:
    keys = jax.random.split(jax.random.key(seed), 8)
    return {
        "gate_act": gaussian(keys[0], (TOKENS, D), 1.0, 6.0, ((0, 32), (1, 16))),
        "key_act": gaussian(keys[1], (TOKENS, D), 1.0, 6.0, ((0, 32), (1, 16))),
        "value_act": gaussian(keys[2], (TOKENS, D), 1.0, 6.0, ((0, 32), (1, 16))),
        "decay_rate": jnp.clip(jnp.exp(math.log(0.05) - 7.4014754 * jax.random.uniform(keys[3], (D, MODES), jnp.float32) ** level_of(keys[3], (D, MODES), ((0, 16),), -0.2, 0.2)), 3.0517578125e-05, 0.05),
        "residue": gaussian(keys[4], (D, MODES), 0.25, 1.5, ((0, 16),), jnp.float32),
        "skip": jnp.clip(0.5 + 1.0 * jax.random.uniform(keys[5], (D,), jnp.float32) ** level_of(keys[5], (D,), ((0, 16),), -0.2, 0.2), 0.5, 1.5),
        "out_weight": gaussian(keys[6], (D, D), D ** -0.5, 0.09375, ((1, 16),)),
    }


def channel_block(inputs):
    signal, rates, weights = inputs
    length = signal.shape[1]
    steps = jnp.arange(length).astype(jnp.float32)
    impulse = jnp.zeros(signal.shape, jnp.float32)
    for mode in range(MODES):
        coef = weights[:, mode] * jnp.sqrt(2.0 * rates[:, mode])
        impulse = impulse + coef[:, None] * jnp.exp(-(rates[:, mode][:, None] * steps[None, :]))
    spec_signal = jnp.fft.rfft(signal.astype(jnp.float32), n=2 * length, axis=1)
    spec_filter = jnp.fft.rfft(impulse, n=2 * length, axis=1)
    return jnp.fft.irfft(spec_signal * spec_filter, n=2 * length, axis=1)[:, :length]

def reference(gate_act, key_act, value_act, decay_rate, residue, skip, out_weight):
    mixed = (key_act.astype(jnp.float32) * value_act.astype(jnp.float32)).astype(jnp.bfloat16)
    group = 256
    blocks = D // group
    signal = mixed.T.reshape(blocks, group, TOKENS)
    rates = decay_rate.reshape(blocks, group, MODES)
    weights = residue.reshape(blocks, group, MODES)
    conv = lax.map(channel_block, (signal, rates, weights)).reshape(D, TOKENS).T
    gated = (gate_act.astype(jnp.float32) * (conv + skip[None, :] * mixed.astype(jnp.float32))).astype(jnp.bfloat16)
    return jnp.dot(gated, out_weight, preferred_element_type=jnp.float32).astype(jnp.bfloat16)
```

```python
import functools

import jax
import jax.numpy as jnp
from jax import lax
from jax.experimental import pallas as pl
from jax.experimental.pallas import tpu as pltpu
from jax.sharding import PartitionSpec as P

CHUNKS = 8
LANES = 128
Z, Y, CORES, X = 16, 4, 2, 4
LOW = Z // 2
AXES = ("tensor", "context")


def linear(x, y, z, core):
    x, y, z, core = x % X, y % Y, z % Z, core % CORES
    tensor = (z // LOW * Y + y) * CORES + core
    return tensor * (X * LOW) + x * LOW + z % LOW


def move(array, dy=0, dz=0, dcore=0):
    pairs = []
    for x in range(X):
        for y in range(Y):
            for z in range(Z):
                for core in range(CORES):
                    way = 1 if core == 0 else -1
                    pairs.append((linear(x, y, z, core), linear(x, y + dy, z + way * dz, core + dcore)))
    return lax.ppermute(array, AXES, pairs)


def fill_mixed(key_ref, value_ref, x_scr):
    product = key_ref[...].astype(jnp.float32) * value_ref[...].astype(jnp.float32)
    mixed = product.astype(jnp.bfloat16).astype(jnp.float32)
    for half in range(x_scr.shape[0]):
        x_scr[half] = mixed[:, half * LANES : (half + 1) * LANES]


def shifted(values, by):
    rows = lax.broadcasted_iota(jnp.int32, values.shape, 0)
    return jnp.where(rows >= by, pltpu.roll(values, by, 0), 0.0)


def ends_kernel(key_ref, value_ref, decay_ref, ends_ref, prefix_ref, x_scr, e_scr):
    fill_mixed(key_ref, value_ref, x_scr)
    tokens = x_scr.shape[1]
    length = tokens // CHUNKS
    rates = decay_ref[...].T
    modes = rates.shape[0]
    for half in range(x_scr.shape[0]):
        cols = slice(half * LANES, (half + 1) * LANES)
        rate = [jnp.broadcast_to(rates[m : m + 1, cols], (CHUNKS, LANES)) for m in range(modes)]
        decay = [jnp.exp(-r) for r in rate]

        def step(t, states):
            x = x_scr[half, pl.ds(t, CHUNKS, stride=length), :]
            return tuple(decay[m] * states[m] + x for m in range(modes))

        zero = jnp.zeros((CHUNKS, LANES), jnp.float32)
        states = lax.fori_loop(0, length, step, (zero,) * modes, unroll=4)
        for m in range(modes):
            total = states[m]
            by = 1
            while by < CHUNKS:
                total = total + jnp.exp(-(rate[m] * float(length * by))) * shifted(total, by)
                by *= 2
            prefix_ref[m, :, cols] = shifted(total, 1)
            e_scr[m : m + 1, cols] = total[CHUNKS - 1 : CHUNKS, :]
    ends_ref[...] = jnp.broadcast_to(e_scr[...].astype(jnp.bfloat16)[None], ends_ref.shape)


def conv_kernel(
    place_ref, gate_ref, key_ref, value_ref, decay_ref, residue_ref, skip_ref, prefix_ref, ends_ref, out_ref, x_scr, y_scr
):
    fill_mixed(key_ref, value_ref, x_scr)
    tokens = x_scr.shape[1]
    length = tokens // CHUNKS
    rates = decay_ref[...].T
    coefs = residue_ref[...].T * jnp.sqrt(2.0 * rates)
    modes = rates.shape[0]
    place = place_ref[0]
    whole = jnp.exp(-(rates * float(tokens)))

    def join(q, carried):
        return jnp.where(q < place, whole * carried + ends_ref[q].astype(jnp.float32), carried)

    carried = lax.fori_loop(0, ends_ref.shape[0], join, jnp.zeros_like(rates), unroll=4)
    row = lax.broadcasted_iota(jnp.int32, (CHUNKS, LANES), 0).astype(jnp.float32) * float(length)
    for half in range(x_scr.shape[0]):
        cols = slice(half * LANES, (half + 1) * LANES)

        def wide(values, m):
            return jnp.broadcast_to(values[m : m + 1, cols], (CHUNKS, LANES))

        rate = [wide(rates, m) for m in range(modes)]
        decay = [jnp.exp(-r) for r in rate]
        coef = [wide(coefs, m) for m in range(modes)]
        skip = jnp.broadcast_to(skip_ref[:, cols], (CHUNKS, LANES))
        first = tuple(prefix_ref[m, :, cols] + jnp.exp(-(rate[m] * row)) * wide(carried, m) for m in range(modes))

        def step(t, states):
            x = x_scr[half, pl.ds(t, CHUNKS, stride=length), :]
            states = tuple(decay[m] * states[m] + x for m in range(modes))
            terms = [coef[m] * states[m] for m in range(modes)]
            while len(terms) > 1:
                terms = [a + b for a, b in zip(terms[::2], terms[1::2])]
            y_scr[half, pl.ds(t, CHUNKS, stride=length), :] = terms[0] + skip * x
            return states

        lax.fori_loop(0, length, step, first, unroll=2)
        out_ref[:, cols] = (gate_ref[:, cols].astype(jnp.float32) * y_scr[half]).astype(jnp.bfloat16)


def pick_kernel(order_ref, keep_in, send_in, keep_out, send_out):
    keep_out[...] = keep_in[...]
    send_out[...] = send_in[...]


def first_product(p0, p1, p2, p3, mine_ref, other_ref, mine_out, other_out):
    for weight, out in ((mine_ref, mine_out), (other_ref, other_out)):
        total = jnp.dot(p0[...], weight[0], preferred_element_type=jnp.float32)
        for i, piece in enumerate((p1, p2, p3)):
            total += jnp.dot(piece[...], weight[i + 1], preferred_element_type=jnp.float32)
        out[...] = total


def second_product(p0, p1, p2, p3, mine_ref, other_ref, mine_in, other_in, mine_out, other_out):
    for weight, start, out in ((other_ref, other_in, other_out), (mine_ref, mine_in, mine_out)):
        total = start[...]
        for i, piece in enumerate((p0, p1, p2, p3)):
            total += jnp.dot(piece[...], weight[i], preferred_element_type=jnp.float32)
        out[...] = total.astype(out.dtype)


def full(array):
    rank = len(array.shape)
    return pl.BlockSpec(array.shape, lambda *_: (0,) * rank)


PARAMS = pltpu.CompilerParams(vmem_limit_bytes=40 * 1024 * 1024)


def call(kernel, args, outs, scratch=(), flops=0, scalars=0):
    in_specs = [pl.BlockSpec(memory_space=pltpu.SMEM)] * scalars + [full(a) for a in args[scalars:]]
    moved = sum(a.size * a.dtype.itemsize for a in (*args, *outs))
    return pl.pallas_call(
        kernel,
        grid=(1,),
        in_specs=in_specs,
        out_specs=[full(o) for o in outs],
        out_shape=list(outs),
        scratch_shapes=list(scratch),
        compiler_params=PARAMS,
        cost_estimate=pl.CostEstimate(flops=flops, bytes_accessed=moved, transcendentals=0),
    )(*args)


def body(gate_act, key_act, value_act, decay_rate, residue, skip, out_weight):
    tokens, width = gate_act.shape
    modes = decay_rate.shape[1]
    parts = lax.axis_size("context")
    place = lax.axis_index("context")
    here = lax.axis_index("tensor")
    z_hi, y, core = here // (Y * CORES), here // CORES % Y, here % CORES
    shape = jax.ShapeDtypeStruct
    f32, bf16 = jnp.float32, jnp.bfloat16
    halves = width // LANES
    block = pltpu.VMEM((halves, tokens, LANES), f32)

    ends, prefix = call(
        ends_kernel,
        (key_act, value_act, decay_rate),
        (shape((parts, modes, width), bf16), shape((modes, CHUNKS, width), f32)),
        (block, pltpu.VMEM((modes, width), f32)),
        flops=2 * tokens * width * modes,
    )
    with jax.named_scope("block_states"):
        ends = lax.all_to_all(ends, "context", 0, 0)

    ys = jnp.stack([y, (y - 1) % Y, (y + 1) % Y, (y + 2) % Y])
    rows = jnp.concatenate([z_hi * Y + ys, (1 - z_hi) * Y + ys])
    order = jnp.stack([rows * CORES + core, rows * CORES + 1 - core]).astype(jnp.int32)
    slab = (1, width, out_weight.shape[1])
    pieces = rows.shape[0]
    picked = shape((pieces, *slab[1:]), bf16)
    by_rows = out_weight.reshape(2 * pieces, *slab[1:])
    mine, theirs = pl.pallas_call(
        pick_kernel,
        grid_spec=pltpu.PrefetchScalarGridSpec(
            num_scalar_prefetch=1,
            grid=(pieces,),
            in_specs=[
                pl.BlockSpec(slab, lambda i, order: (order[0, i], 0, 0)),
                pl.BlockSpec(slab, lambda i, order: (order[1, i], 0, 0)),
            ],
            out_specs=[pl.BlockSpec(slab, lambda i, order: (i, 0, 0))] * 2,
        ),
        out_shape=[picked, picked],
        compiler_params=PARAMS,
    )(order, by_rows, by_rows)
    with jax.named_scope("weight_swap"):
        other = move(theirs, dcore=1)

    (gated,) = call(
        conv_kernel,
        (place.reshape(1), gate_act, key_act, value_act, decay_rate, residue, skip.reshape(1, width), prefix, ends),
        (shape((tokens, width), bf16),),
        (block, block),
        flops=4 * tokens * width * modes,
        scalars=1,
    )

    with jax.named_scope("along_z"):
        far = move(gated, dz=Z // 2 - 1)
    with jax.named_scope("own_along_y"):
        near = [gated] + [move(gated, dy=d) for d in (1, -1, 2)]
    sums = shape((tokens, out_weight.shape[1]), f32)
    work = 2 * 2 * tokens * (pieces // 2) * width * out_weight.shape[1]
    half = pieces // 2
    mine_sum, other_sum = call(first_product, (*near, mine[:half], other[:half]), (sums, sums), flops=work)
    with jax.named_scope("far_along_y"):
        far = [move(far, dy=d, dz=1) for d in (0, 1, -1, 2)]
    mine_sum, other_sum = call(
        second_product,
        (*far, mine[half:], other[half:], mine_sum, other_sum),
        (sums, shape(sums.shape, bf16)),
        flops=work,
    )
    with jax.named_scope("sum_swap"):
        from_other = move(other_sum, dcore=1)
    return (mine_sum + from_other.astype(f32)).astype(bf16)


def solution(mesh):
    in_specs = (
        P("context", "tensor"),
        P("context", "tensor"),
        P("context", "tensor"),
        P("tensor", None),
        P("tensor", None),
        P("tensor"),
        P(None, "tensor"),
    )
    return jax.shard_map(body, mesh=mesh, in_specs=in_specs, out_specs=P("context", "tensor"), check_vma=False)
```

```python
import jax
import jax.numpy as jnp
from jax import lax
from jax.experimental import pallas as pl
from jax.experimental.pallas import tpu as pltpu
from jax.sharding import PartitionSpec as P

CHUNKS = 8
LANES = 128
Z, Y, CORES, X = 16, 4, 2, 4
LOW = Z // 2
AXES = ("tensor", "context")


def linear(x, y, z, core):
    x, y, z, core = x % X, y % Y, z % Z, core % CORES
    tensor = (z // LOW * Y + y) * CORES + core
    return tensor * (X * LOW) + x * LOW + z % LOW


def move(array, dy=0, dz=0, dcore=0):
    pairs = []
    for x in range(X):
        for y in range(Y):
            for z in range(Z):
                for core in range(CORES):
                    pairs.append((linear(x, y, z, core), linear(x, y + dy, z + dz, core + dcore)))
    return lax.ppermute(array, AXES, pairs)


def mixed_of(key_ref, value_ref):
    product = key_ref[...].astype(jnp.float32) * value_ref[...].astype(jnp.float32)
    return product.astype(jnp.bfloat16).astype(jnp.float32)


def shifted(values, by):
    rows = lax.broadcasted_iota(jnp.int32, values.shape, 0)
    return jnp.where(rows >= by, pltpu.roll(values, by, 0), 0.0)


def ends_kernel(key_ref, value_ref, decay_ref, ends_ref, states_ref, x_scr, e_scr):
    x_scr[...] = mixed_of(key_ref, value_ref)
    length = x_scr.shape[0] // CHUNKS
    modes = decay_ref.shape[0]
    rate = [jnp.broadcast_to(decay_ref[m : m + 1, :], (CHUNKS, LANES)) for m in range(modes)]
    decay = [jnp.exp(-r) for r in rate]

    def step(t, states):
        x = x_scr[pl.ds(t, CHUNKS, stride=length), :]
        return tuple(decay[m] * states[m] + x for m in range(modes))

    zero = jnp.zeros((CHUNKS, LANES), jnp.float32)
    states = lax.fori_loop(0, length, step, (zero,) * modes, unroll=4)
    later = (CHUNKS - 1 - lax.broadcasted_iota(jnp.int32, (CHUNKS, LANES), 0)).astype(jnp.float32) * float(length)
    for m in range(modes):
        states_ref[m] = states[m]
        e_scr[m : m + 1, :] = jnp.sum(jnp.exp(-(rate[m] * later)) * states[m], axis=0, keepdims=True)
    ends_ref[...] = jnp.broadcast_to(e_scr[...].astype(jnp.bfloat16)[None], ends_ref.shape)


def row_kernel(place_ref, ends_ref, decay_ref, before_ref, row_ref):
    rates = decay_ref[...]
    length = place_ref[1]
    whole = jnp.exp(-(rates * length.astype(jnp.float32)))
    before = total = jnp.zeros_like(rates)
    for q in range(ends_ref.shape[0]):
        end = ends_ref[q].astype(jnp.float32)
        before = jnp.where(q < place_ref[0], whole * before + end, before)
        total = whole * total + end
    before_ref[...] = before
    row_ref[...] = jnp.broadcast_to(total.astype(jnp.bfloat16)[None], row_ref.shape)


def wide(values, m, cols):
    return jnp.broadcast_to(values[m : m + 1, cols], (CHUNKS, LANES))


def add_up(terms):
    while len(terms) > 1:
        terms = [a + b for a, b in zip(terms[::2], terms[1::2])]
    return terms[0]


def local_kernel(gate_ref, key_ref, value_ref, decay_ref, residue_ref, skip_ref, states_ref, local_ref, x_scr, y_scr):
    x_scr[...] = mixed_of(key_ref, value_ref)
    tokens = x_scr.shape[0]
    length = tokens // CHUNKS
    rates = decay_ref[...]
    coefs = residue_ref[...] * jnp.sqrt(2.0 * rates)
    modes = rates.shape[0]
    rate = [jnp.broadcast_to(rates[m : m + 1, :], (CHUNKS, LANES)) for m in range(modes)]
    decay = [jnp.exp(-r) for r in rate]
    coef = [jnp.broadcast_to(coefs[m : m + 1, :], (CHUNKS, LANES)) for m in range(modes)]
    skip = jnp.broadcast_to(skip_ref[...], (CHUNKS, LANES))
    first = []
    for m in range(modes):
        total = states_ref[m]
        by = 1
        while by < CHUNKS:
            total = total + jnp.exp(-(rate[m] * float(length * by))) * shifted(total, by)
            by *= 2
        first.append(shifted(total, 1))

    def step(t, states):
        x = x_scr[pl.ds(t, CHUNKS, stride=length), :]
        states = tuple(decay[m] * states[m] + x for m in range(modes))
        total = add_up([coef[m] * states[m] for m in range(modes)])
        y_scr[pl.ds(t, CHUNKS, stride=length), :] = total + skip * x
        return states

    lax.fori_loop(0, length, step, tuple(first), unroll=2)
    local_ref[:tokens, :] = gate_ref[...].astype(jnp.float32) * y_scr[...]
    local_ref[tokens : tokens + modes, :] = rates
    local_ref[tokens + modes :, :] = coefs


def from_states(rates, start, y_scr, rows):
    modes = rates.shape[0]
    after = lax.broadcasted_iota(jnp.int32, (CHUNKS, LANES), 0).astype(jnp.float32) + 1.0
    for half in range(y_scr.shape[0]):
        cols = slice(half * LANES, (half + 1) * LANES)
        rate = [wide(rates, m, cols) for m in range(modes)]
        decay = [jnp.exp(-(r * float(CHUNKS))) for r in rate]
        first = tuple(wide(start, m, cols) * jnp.exp(-(rate[m] * after)) for m in range(modes))

        def step(g, terms):
            y_scr[half, pl.ds(pl.multiple_of(g * CHUNKS, CHUNKS), CHUNKS), :] = add_up(list(terms))
            return tuple(decay[m] * terms[m] for m in range(modes))

        lax.fori_loop(0, rows // CHUNKS, step, first, unroll=4)


def carry_kernel(place_ref, rows_ref, before_ref, local_ref, gate_hbm, gated_ref, y_scr, gate_ref, arrived):
    fetch = pltpu.make_async_copy(gate_hbm, gate_ref, arrived)
    fetch.start()
    tokens = y_scr.shape[1]
    modes = (local_ref.shape[0] - tokens) // 2
    rates, coefs = local_ref[tokens : tokens + modes, :], local_ref[tokens + modes :, :]
    row, here, length = place_ref[0], place_ref[1], place_ref[2]
    whole = jnp.exp(-(rates * length.astype(jnp.float32)))
    carried = jnp.zeros_like(rates)
    for q in range(rows_ref.shape[0]):
        carried = jnp.where(q < row, whole * carried + rows_ref[q].astype(jnp.float32), carried)
    start = coefs * (before_ref[...] + jnp.exp(-(rates * here.astype(jnp.float32))) * carried)
    from_states(rates, start, y_scr, tokens)
    fetch.wait()
    for half in range(y_scr.shape[0]):
        cols = slice(half * LANES, (half + 1) * LANES)
        gate = gate_ref[:, cols].astype(jnp.float32)
        gated_ref[:, cols] = (local_ref[:tokens, cols] + gate * y_scr[half]).astype(jnp.bfloat16)


def copies_kernel(in_ref, out_ref):
    for i in range(out_ref.shape[0]):
        out_ref[i] = in_ref[...]


def near_product(
    order_ref, p0, p1, p2, p3, mine_hbm, other_hbm, mine_out, other_out, far_mine, far_other, near_mine, near_other, arrived
):
    sides = ((mine_hbm, near_mine, far_mine), (other_hbm, near_other, far_other))

    def copy(side, i):
        source, near, far = sides[side]
        target = near.at[i] if i < Y else far.at[i - Y]
        return pltpu.make_async_copy(source.at[order_ref[i]], target, arrived.at[side, i])

    for i in range(2 * Y):
        for side in range(2):
            copy(side, i).start()
    totals = [0.0, 0.0]
    for i, piece in enumerate((p0, p1, p2, p3)):
        for side in range(2):
            copy(side, i).wait()
            totals[side] += jnp.dot(piece[...], sides[side][1][i], preferred_element_type=jnp.float32)
    mine_out[...], other_out[...] = totals
    for i in range(Y, 2 * Y):
        for side in range(2):
            copy(side, i).wait()


def far_product(pieces_ref, weight_ref, start_ref, out_ref):
    total = start_ref[...]
    for i in range(Y):
        total += jnp.dot(pieces_ref[i], weight_ref[i], preferred_element_type=jnp.float32)
    out_ref[...] = total.astype(out_ref.dtype)


def full(array):
    rank = len(array.shape)
    return pl.BlockSpec(array.shape, lambda *_: (0,) * rank)


def params(mebibytes):
    return pltpu.CompilerParams(vmem_limit_bytes=mebibytes * 1024 * 1024)


def cost(args, outs, flops):
    moved = sum(a.size * a.dtype.itemsize for a in (*args, *outs))
    return pl.CostEstimate(flops=flops, bytes_accessed=moved, transcendentals=0)


def call(kernel, args, outs, scratch=(), flops=0, scalars=0, limit=16, fetched=(), after=()):
    count, waits = len(args) + len(fetched), len(after)

    def run(*refs):
        kernel(*refs[:count], *refs[count + waits :])

    return pl.pallas_call(
        run,
        grid=(1,),
        in_specs=[
            *[pl.BlockSpec(memory_space=pltpu.SMEM)] * scalars,
            *[full(a) for a in args[scalars:]],
            *[pl.BlockSpec(memory_space=pl.ANY)] * (len(fetched) + waits),
        ],
        out_specs=[full(o) for o in outs],
        out_shape=list(outs),
        scratch_shapes=list(scratch),
        compiler_params=params(limit),
        cost_estimate=cost(args, outs, flops),
    )(*args, *fetched, *after)


def body(gate_act, key_act, value_act, decay_rate, residue, skip, out_weight):
    tokens, width = gate_act.shape
    columns = out_weight.shape[1]
    parts = lax.axis_size("context")
    decay_rate, residue, skip = decay_rate.T, residue.T, skip.reshape(1, width)
    modes = decay_rate.shape[0]
    place = lax.axis_index("context")
    here = lax.axis_index("tensor")
    f32, bf16 = jnp.float32, jnp.bfloat16

    def shape(dtype, *dims):
        return jax.ShapeDtypeStruct(dims, dtype)

    halves = width // LANES
    block = pltpu.VMEM((halves, tokens, LANES), f32)

    def by_half(kernel, args, outs, scratch, flops, limit):
        def spec(array):
            lead = array.shape[:-1]
            return pl.BlockSpec((*lead, LANES), lambda h: (*(0 for _ in lead), h))

        return pl.pallas_call(
            kernel,
            grid=(halves,),
            in_specs=[spec(a) for a in args],
            out_specs=[spec(o) for o in outs],
            out_shape=list(outs),
            scratch_shapes=list(scratch),
            compiler_params=params(limit),
            cost_estimate=cost(args, outs, flops),
        )(*args)

    row, spot = place // LOW, place % LOW
    column = pltpu.VMEM((tokens, LANES), f32)
    ends, states = by_half(
        ends_kernel,
        (key_act, value_act, decay_rate),
        (shape(bf16, LOW, modes, width), shape(f32, modes, CHUNKS, width)),
        (column, pltpu.VMEM((modes, LANES), f32)),
        2 * tokens * width * modes,
        58,
    )
    with jax.named_scope("states_along_z"):
        groups = [[x * LOW + z for z in range(LOW)] for x in range(X)]
        ends = lax.all_to_all(ends, "context", 0, 0, axis_index_groups=groups)
    (local,) = by_half(
        local_kernel,
        (gate_act, key_act, value_act, decay_rate, residue, skip, states),
        (shape(f32, tokens + 2 * modes, width),),
        (column, column),
        4 * tokens * width * modes,
        58,
    )
    before, rows = call(
        row_kernel,
        (jnp.stack([spot, jnp.int32(tokens)]), ends, decay_rate),
        (shape(f32, modes, width), shape(bf16, X, modes, width)),
        scalars=1,
    )
    with jax.named_scope("states_along_x"):
        groups = [[x * LOW + z for x in range(X)] for z in range(LOW)]
        rows = lax.all_to_all(rows, "context", 0, 0, axis_index_groups=groups)
    (gated,) = call(
        carry_kernel,
        (jnp.stack([row, spot * tokens, jnp.int32(tokens * LOW)]), rows, before, local),
        (shape(bf16, tokens, width),),
        (block, pltpu.VMEM((tokens, width), bf16), pltpu.SemaphoreType.DMA),
        flops=2 * tokens * width * modes,
        scalars=1,
        fetched=(gate_act,),
    )
    with jax.named_scope("along_z"):
        far = move(gated, dz=Z // 2)
    with jax.named_scope("own_along_y"):
        *near, other_weight = lax.cond(
            place < parts,
            lambda own, weight: (*[move(own, dy=d) for d in (2, 1, -1)], move(weight, dcore=1)),
            lambda own, weight: (own, own, own, weight),
            gated,
            out_weight,
        )
        near = [gated, *near]

    z_hi, y, core = here // (Y * CORES), here // CORES % Y, here % CORES
    ys = jnp.stack([y, (y + 2) % Y, (y - 1) % Y, (y + 1) % Y])
    order = (jnp.concatenate([z_hi * Y + ys, (1 - z_hi) * Y + jnp.arange(Y)]) * CORES + core).astype(jnp.int32)
    blocks = [weight.reshape(2 * Y * CORES, width, columns) for weight in (out_weight, other_weight)]
    sums, picked = shape(f32, tokens, columns), shape(bf16, Y, width, columns)
    mine_sum, other_sum, far_mine, far_other = call(
        near_product,
        (order, *near),
        (sums, sums, picked, picked),
        [pltpu.VMEM(picked.shape, bf16)] * 2 + [pltpu.SemaphoreType.DMA((2, 2 * Y))],
        flops=4 * tokens * Y * width * columns,
        scalars=1,
        fetched=blocks,
    )
    with jax.named_scope("far_along_y"):
        (far,) = call(copies_kernel, (far,), (shape(bf16, Y, tokens, width),), after=(mine_sum,))
        groups = [[(high * Y + y) * CORES + core for y in range(Y)] for high in range(Z // LOW) for core in range(CORES)]
        far = lax.all_to_all(far, "tensor", 0, 0, axis_index_groups=groups)
    work = 2 * tokens * Y * width * columns
    (other_sum,) = call(far_product, (far, far_other, other_sum), (shape(bf16, tokens, columns),), flops=work)
    with jax.named_scope("sum_swap"):
        from_other = move(other_sum, dcore=1)
    (mine_sum,) = call(far_product, (far, far_mine, mine_sum), (sums,), flops=work)
    return (mine_sum + from_other.astype(f32)).astype(bf16)


def solution(mesh):
    in_specs = (
        P("context", "tensor"),
        P("context", "tensor"),
        P("context", "tensor"),
        P("tensor", None),
        P("tensor", None),
        P("tensor"),
        P(None, "tensor"),
    )
    return jax.shard_map(body, mesh=mesh, in_specs=in_specs, out_specs=P("context", "tensor"), check_vma=False)
```

```python
import jax
import jax.numpy as jnp
from jax import lax
from jax.experimental import pallas as pl
from jax.experimental.pallas import tpu as pltpu
from jax.sharding import PartitionSpec as P

CHUNKS = 8
LANES = 128
Z, Y, CORES, X = 16, 4, 2, 4
LOW = Z // 2
AXES = ("tensor", "context")


def linear(x, y, z, core):
    x, y, z, core = x % X, y % Y, z % Z, core % CORES
    tensor = (z // LOW * Y + y) * CORES + core
    return tensor * (X * LOW) + x * LOW + z % LOW


def move(array, dy=0, dz=0, dcore=0):
    pairs = []
    for x in range(X):
        for y in range(Y):
            for z in range(Z):
                for core in range(CORES):
                    pairs.append((linear(x, y, z, core), linear(x, y + dy, z + dz, core + dcore)))
    return lax.ppermute(array, AXES, pairs)


def mixed_of(key_ref, value_ref):
    product = key_ref[...].astype(jnp.float32) * value_ref[...].astype(jnp.float32)
    return product.astype(jnp.bfloat16).astype(jnp.float32)


def shifted(values, by):
    rows = lax.broadcasted_iota(jnp.int32, values.shape, 0)
    return jnp.where(rows >= by, pltpu.roll(values, by, 0), 0.0)


def ends_kernel(spot_ref, key_ref, value_ref, decay_ref, ends_ref, states_ref, x_scr, e_scr):
    x_scr[...] = mixed_of(key_ref, value_ref)
    length = x_scr.shape[0] // CHUNKS
    modes = decay_ref.shape[0]
    rate = [jnp.broadcast_to(decay_ref[m : m + 1, :], (CHUNKS, LANES)) for m in range(modes)]
    decay = [jnp.exp(-r) for r in rate]

    def step(t, states):
        x = x_scr[pl.ds(t, CHUNKS, stride=length), :]
        return tuple(decay[m] * states[m] + x for m in range(modes))

    zero = jnp.zeros((CHUNKS, LANES), jnp.float32)
    states = lax.fori_loop(0, length, step, (zero,) * modes, unroll=4)
    later = (CHUNKS - 1 - lax.broadcasted_iota(jnp.int32, (CHUNKS, LANES), 0)).astype(jnp.float32) * float(length)
    for m in range(modes):
        states_ref[m] = states[m]
        e_scr[m : m + 1, :] = jnp.sum(jnp.exp(-(rate[m] * later)) * states[m], axis=0, keepdims=True)
    spot, end, rates = spot_ref[0], e_scr[...], decay_ref[...]
    for q in range(ends_ref.shape[0]):
        to_row = jnp.maximum(q - 1 - spot, 0).astype(jnp.float32) * float(x_scr.shape[0])
        to_next = (q + ends_ref.shape[0] - 1 - spot).astype(jnp.float32) * float(x_scr.shape[0])
        ends_ref[q, :modes, :] = jnp.where(spot < q, jnp.exp(-(rates * to_row)) * end, 0.0).astype(jnp.bfloat16)
        ends_ref[q, modes:, :] = (jnp.exp(-(rates * to_next)) * end).astype(jnp.bfloat16)


def row_kernel(ends_ref, before_ref, row_ref):
    modes = before_ref.shape[0]
    total = ends_ref[0].astype(jnp.float32)
    for q in range(1, ends_ref.shape[0]):
        total += ends_ref[q].astype(jnp.float32)
    before_ref[...] = total[:modes, :]
    row_ref[...] = jnp.broadcast_to(total[modes:, :].astype(jnp.bfloat16)[None], row_ref.shape)


def wide(values, m, cols):
    return jnp.broadcast_to(values[m : m + 1, cols], (CHUNKS, LANES))


def add_up(terms):
    while len(terms) > 1:
        terms = [a + b for a, b in zip(terms[::2], terms[1::2])]
    return terms[0]


def local_kernel(gate_ref, key_ref, value_ref, modal_ref, states_ref, local_ref, x_scr, y_scr):
    mixed = mixed_of(key_ref, value_ref)
    tokens = x_scr.shape[1]
    length = tokens // CHUNKS
    modes = states_ref.shape[0]
    rates = modal_ref[:modes, :]
    coefs = modal_ref[modes : 2 * modes, :] * jnp.sqrt(2.0 * rates)
    for half in range(x_scr.shape[0]):
        cols = slice(half * LANES, (half + 1) * LANES)
        x_scr[half] = mixed[:, cols]
        rate = [wide(rates, m, cols) for m in range(modes)]
        decay = [jnp.exp(-r) for r in rate]
        coef = [wide(coefs, m, cols) for m in range(modes)]
        skip = wide(modal_ref[2 * modes : 2 * modes + 1, :], 0, cols)
        first = []
        for m in range(modes):
            total = states_ref[m, :, cols]
            by = 1
            while by < CHUNKS:
                total = total + jnp.exp(-(rate[m] * float(length * by))) * shifted(total, by)
                by *= 2
            first.append(shifted(total, 1))

        def step(t, states):
            x = x_scr[half, pl.ds(t, CHUNKS, stride=length), :]
            states = tuple(decay[m] * states[m] + x for m in range(modes))
            total = add_up([coef[m] * states[m] for m in range(modes)])
            y_scr[half, pl.ds(t, CHUNKS, stride=length), :] = total + skip * x
            return states

        lax.fori_loop(0, length, step, tuple(first), unroll=2)
        local_ref[:tokens, cols] = gate_ref[:, cols].astype(jnp.float32) * y_scr[half]
    local_ref[tokens : tokens + modes, :] = rates
    local_ref[tokens + modes :, :] = coefs


def from_states(rates, start, y_scr, rows):
    modes = rates.shape[0]
    after = lax.broadcasted_iota(jnp.int32, (CHUNKS, LANES), 0).astype(jnp.float32) + 1.0
    for half in range(y_scr.shape[0]):
        cols = slice(half * LANES, (half + 1) * LANES)
        rate = [wide(rates, m, cols) for m in range(modes)]
        decay = [jnp.exp(-(r * float(CHUNKS))) for r in rate]
        first = tuple(wide(start, m, cols) * jnp.exp(-(rate[m] * after)) for m in range(modes))

        def step(g, terms):
            y_scr[half, pl.ds(pl.multiple_of(g * CHUNKS, CHUNKS), CHUNKS), :] = add_up(list(terms))
            return tuple(decay[m] * terms[m] for m in range(modes))

        lax.fori_loop(0, rows // CHUNKS, step, first, unroll=4)


def carry_kernel(place_ref, rows_ref, before_ref, local_ref, gate_hbm, gated_ref, y_scr, gate_ref, arrived):
    fetch = pltpu.make_async_copy(gate_hbm, gate_ref, arrived)
    fetch.start()
    tokens = y_scr.shape[1]
    modes = (local_ref.shape[0] - tokens) // 2
    rates, coefs = local_ref[tokens : tokens + modes, :], local_ref[tokens + modes :, :]
    row, length = place_ref[0], place_ref[1]
    whole = jnp.exp(-(rates * length.astype(jnp.float32)))
    carried = jnp.zeros_like(rates)
    for q in range(rows_ref.shape[0]):
        carried = jnp.where(q < row, whole * carried + rows_ref[q].astype(jnp.float32), carried)
    start = coefs * (before_ref[...] + carried)
    from_states(rates, start, y_scr, tokens)
    fetch.wait()
    for half in range(y_scr.shape[0]):
        cols = slice(half * LANES, (half + 1) * LANES)
        gate = gate_ref[:, cols].astype(jnp.float32)
        gated_ref[:, cols] = (local_ref[:tokens, cols] + gate * y_scr[half]).astype(jnp.bfloat16)


def copies_kernel(in_ref, out_ref):
    for i in range(out_ref.shape[0]):
        out_ref[i] = in_ref[...]


def near_product(order_ref, p0, p1, p2, p3, mine_ref, other_ref, mine_out, other_out, far_mine, far_other):
    for weight, out, far in ((mine_ref, mine_out, far_mine), (other_ref, other_out, far_other)):
        total = jnp.zeros(out.shape, jnp.float32)
        for i, piece in enumerate((p0, p1, p2, p3)):
            total += jnp.dot(piece[...], block_of(weight, order_ref[i]), preferred_element_type=jnp.float32)
        out[...] = total
        for i in range(Y):
            far[i] = block_of(weight, order_ref[Y + i])


def block_of(weight_ref, index):
    height = weight_ref.shape[0] // (2 * Y * CORES)
    return weight_ref[pl.ds(pl.multiple_of(index * height, height), height), :]


def far_product(pieces_ref, weight_ref, start_ref, out_ref):
    total = start_ref[...]
    for i in range(Y):
        total += jnp.dot(pieces_ref[i], weight_ref[i], preferred_element_type=jnp.float32)
    out_ref[...] = total.astype(out_ref.dtype)


def full(array):
    rank = len(array.shape)
    return pl.BlockSpec(array.shape, lambda *_: (0,) * rank)


def params(mebibytes):
    return pltpu.CompilerParams(vmem_limit_bytes=mebibytes * 1024 * 1024)


def cost(args, outs, flops):
    moved = sum(a.size * a.dtype.itemsize for a in (*args, *outs))
    return pl.CostEstimate(flops=flops, bytes_accessed=moved, transcendentals=0)


def call(kernel, args, outs, scratch=(), flops=0, scalars=0, limit=16, fetched=(), after=()):
    count, waits = len(args) + len(fetched), len(after)

    def run(*refs):
        kernel(*refs[:count], *refs[count + waits :])

    return pl.pallas_call(
        run,
        grid=(1,),
        in_specs=[
            *[pl.BlockSpec(memory_space=pltpu.SMEM)] * scalars,
            *[full(a) for a in args[scalars:]],
            *[pl.BlockSpec(memory_space=pl.ANY)] * (len(fetched) + waits),
        ],
        out_specs=[full(o) for o in outs],
        out_shape=list(outs),
        scratch_shapes=list(scratch),
        compiler_params=params(limit),
        cost_estimate=cost(args, outs, flops),
    )(*args, *fetched, *after)


def body(gate_act, key_act, value_act, decay_rate, residue, skip, out_weight):
    tokens, width = gate_act.shape
    columns = out_weight.shape[1]
    parts = lax.axis_size("context")
    decay_rate, residue, skip = decay_rate.T, residue.T, skip.reshape(1, width)
    modes = decay_rate.shape[0]
    place = lax.axis_index("context")
    here = lax.axis_index("tensor")
    f32, bf16 = jnp.float32, jnp.bfloat16

    def shape(dtype, *dims):
        return jax.ShapeDtypeStruct(dims, dtype)

    halves = width // LANES
    block = pltpu.VMEM((halves, tokens, LANES), f32)

    row, spot = place // LOW, place % LOW
    ends_out = (shape(bf16, LOW, 2 * modes, width), shape(f32, modes, CHUNKS, width))
    ends, states = pl.pallas_call(
        ends_kernel,
        grid=(halves,),
        in_specs=[
            pl.BlockSpec(memory_space=pltpu.SMEM),
            *[pl.BlockSpec((rows, LANES), lambda h: (0, h)) for rows in (tokens, tokens, modes)],
        ],
        out_specs=[pl.BlockSpec((*out.shape[:2], LANES), lambda h: (0, 0, h)) for out in ends_out],
        out_shape=list(ends_out),
        scratch_shapes=[pltpu.VMEM((tokens, LANES), f32), pltpu.VMEM((modes, LANES), f32)],
        compiler_params=params(58),
        cost_estimate=cost((key_act, value_act), ends_out, 2 * tokens * width * modes),
    )(spot.reshape(1), key_act, value_act, decay_rate)
    with jax.named_scope("states_along_z"):
        groups = [[x * LOW + z for z in range(LOW)] for x in range(X)]
        ends = lax.all_to_all(ends, "context", 0, 0, axis_index_groups=groups)
    (local,) = call(
        local_kernel,
        (gate_act, key_act, value_act, jnp.concatenate([decay_rate, residue, skip]), states),
        (shape(f32, tokens + 2 * modes, width),),
        (block, block),
        flops=4 * tokens * width * modes,
    )
    before, rows = call(
        row_kernel, (ends,), (shape(f32, modes, width), shape(bf16, X, modes, width)), after=(local,)
    )
    with jax.named_scope("states_along_x"):
        groups = [[x * LOW + z for x in range(X)] for z in range(LOW)]
        rows = lax.all_to_all(rows, "context", 0, 0, axis_index_groups=groups)
    (gated,) = call(
        carry_kernel,
        (jnp.stack([row, jnp.int32(tokens * LOW)]), rows, before, local),
        (shape(bf16, tokens, width),),
        (block, pltpu.VMEM((tokens, width), bf16), pltpu.SemaphoreType.DMA),
        flops=2 * tokens * width * modes,
        scalars=1,
        fetched=(gate_act,),
    )
    with jax.named_scope("along_z"):
        far = move(gated, dz=Z // 2)
    with jax.named_scope("own_along_y"):
        *near, other_weight = lax.cond(
            place < parts,
            lambda own, weight: (*[move(own, dy=d) for d in (2, 1, -1)], move(weight, dcore=1)),
            lambda own, weight: (own, own, own, weight),
            gated,
            out_weight,
        )
        near = [gated, *near]

    z_hi, y, core = here // (Y * CORES), here // CORES % Y, here % CORES
    ys = jnp.stack([y, (y + 2) % Y, (y - 1) % Y, (y + 1) % Y])
    order = (jnp.concatenate([z_hi * Y + ys, (1 - z_hi) * Y + jnp.arange(Y)]) * CORES + core).astype(jnp.int32)
    sums = shape(f32, tokens, columns)
    work = 2 * tokens * Y * width * columns
    picked = shape(bf16, Y, width, columns)
    mine_sum, other_sum, far_mine, far_other = call(
        near_product,
        (order, *near, out_weight, other_weight),
        (sums, sums, picked, picked),
        flops=2 * work,
        scalars=1,
    )
    with jax.named_scope("far_along_y"):
        (far,) = call(copies_kernel, (far,), (shape(bf16, Y, tokens, width),), after=(mine_sum,))
        groups = [[(high * Y + y) * CORES + core for y in range(Y)] for high in range(Z // LOW) for core in range(CORES)]
        far = lax.all_to_all(far, "tensor", 0, 0, axis_index_groups=groups)
    (other_sum,) = call(far_product, (far, far_other, other_sum), (shape(bf16, tokens, columns),), flops=work)
    with jax.named_scope("sum_swap"):
        from_other = move(other_sum, dcore=1)
    (mine_sum,) = call(far_product, (far, far_mine, mine_sum), (sums,), flops=work)
    return (mine_sum + from_other.astype(f32)).astype(bf16)


def solution(mesh):
    in_specs = (
        P("context", "tensor"),
        P("context", "tensor"),
        P("context", "tensor"),
        P("tensor", None),
        P("tensor", None),
        P("tensor"),
        P(None, "tensor"),
    )
    return jax.shard_map(body, mesh=mesh, in_specs=in_specs, out_specs=P("context", "tensor"), check_vma=False)
```

```python
import jax
import jax.numpy as jnp
from jax import lax
from jax.experimental import pallas as pl
from jax.experimental.pallas import tpu as pltpu
from jax.sharding import PartitionSpec as P

CHUNKS = 8
LANES = 128
Z, Y, CORES, X = 16, 4, 2, 4
LOW = Z // 2
AWAY = (0, 2, 1, -1)
AXES = ("tensor", "context")


def linear(x, y, z, core):
    x, y, z, core = x % X, y % Y, z % Z, core % CORES
    tensor = (z // LOW * Y + y) * CORES + core
    return tensor * (X * LOW) + x * LOW + z % LOW


def move(array, dy=0, dz=0, dcore=0):
    pairs = []
    for x in range(X):
        for y in range(Y):
            for z in range(Z):
                for core in range(CORES):
                    pairs.append((linear(x, y, z, core), linear(x, y + dy, z + dz, core + dcore)))
    return lax.ppermute(array, AXES, pairs)


def mixed_of(key_ref, value_ref):
    product = key_ref[...].astype(jnp.float32) * value_ref[...].astype(jnp.float32)
    return product.astype(jnp.bfloat16).astype(jnp.float32)


def shifted(values, by):
    rows = lax.broadcasted_iota(jnp.int32, values.shape, 0)
    return jnp.where(rows >= by, pltpu.roll(values, by, 0), 0.0)


def ends_kernel(key_ref, value_ref, decay_ref, ends_ref, states_ref, x_scr, e_scr):
    x_scr[...] = mixed_of(key_ref, value_ref)
    length = x_scr.shape[0] // CHUNKS
    modes = decay_ref.shape[0]
    rate = [jnp.broadcast_to(decay_ref[m : m + 1, :], (CHUNKS, LANES)) for m in range(modes)]
    decay = [jnp.exp(-r) for r in rate]

    def step(t, states):
        x = x_scr[pl.ds(t, CHUNKS, stride=length), :]
        return tuple(decay[m] * states[m] + x for m in range(modes))

    zero = jnp.zeros((CHUNKS, LANES), jnp.float32)
    states = lax.fori_loop(0, length, step, (zero,) * modes, unroll=4)
    later = (CHUNKS - 1 - lax.broadcasted_iota(jnp.int32, (CHUNKS, LANES), 0)).astype(jnp.float32) * float(length)
    for m in range(modes):
        states_ref[m] = states[m]
        e_scr[m : m + 1, :] = jnp.sum(jnp.exp(-(rate[m] * later)) * states[m], axis=0, keepdims=True)
    spot = lax.rem(lax.axis_index("context"), LOW)
    end, rates = e_scr[...], decay_ref[...]
    for q in range(ends_ref.shape[0]):
        to_row = jnp.maximum(q - 1 - spot, 0).astype(jnp.float32) * float(x_scr.shape[0])
        to_next = (q + ends_ref.shape[0] - 1 - spot).astype(jnp.float32) * float(x_scr.shape[0])
        ends_ref[q, :modes, :] = jnp.where(spot < q, jnp.exp(-(rates * to_row)) * end, 0.0).astype(jnp.bfloat16)
        ends_ref[q, modes:, :] = (jnp.exp(-(rates * to_next)) * end).astype(jnp.bfloat16)


def row_kernel(ends_ref, before_ref, row_ref):
    modes = before_ref.shape[0]
    total = ends_ref[0].astype(jnp.float32)
    for q in range(1, ends_ref.shape[0]):
        total += ends_ref[q].astype(jnp.float32)
    before_ref[...] = total[:modes, :]
    row_ref[...] = jnp.broadcast_to(total[modes:, :].astype(jnp.bfloat16)[None], row_ref.shape)


def wide(values, m, cols):
    return jnp.broadcast_to(values[m : m + 1, cols], (CHUNKS, LANES))


def add_up(terms):
    while len(terms) > 1:
        terms = [a + b for a, b in zip(terms[::2], terms[1::2])]
    return terms[0]


def local_kernel(gate_ref, key_ref, value_ref, modal_ref, states_ref, local_ref, x_scr, y_scr):
    mixed = mixed_of(key_ref, value_ref)
    tokens = x_scr.shape[1]
    length = tokens // CHUNKS
    modes = states_ref.shape[0]
    rates = modal_ref[:modes, :]
    coefs = modal_ref[modes : 2 * modes, :] * jnp.sqrt(2.0 * rates)
    for half in range(x_scr.shape[0]):
        cols = slice(half * LANES, (half + 1) * LANES)
        x_scr[half] = mixed[:, cols]
        rate = [wide(rates, m, cols) for m in range(modes)]
        decay = [jnp.exp(-r) for r in rate]
        coef = [wide(coefs, m, cols) for m in range(modes)]
        skip = wide(modal_ref[2 * modes : 2 * modes + 1, :], 0, cols)
        first = []
        for m in range(modes):
            total = states_ref[m, :, cols]
            by = 1
            while by < CHUNKS:
                total = total + jnp.exp(-(rate[m] * float(length * by))) * shifted(total, by)
                by *= 2
            first.append(shifted(total, 1))

        def step(t, states):
            x = x_scr[half, pl.ds(t, CHUNKS, stride=length), :]
            states = tuple(decay[m] * states[m] + x for m in range(modes))
            total = add_up([coef[m] * states[m] for m in range(modes)])
            y_scr[half, pl.ds(t, CHUNKS, stride=length), :] = total + skip * x
            return states

        lax.fori_loop(0, length, step, tuple(first), unroll=2)
        local_ref[:tokens, cols] = gate_ref[:, cols].astype(jnp.float32) * y_scr[half]
    local_ref[tokens : tokens + modes, :] = rates
    local_ref[tokens + modes :, :] = coefs


def from_states(rates, start, y_scr, rows):
    modes = rates.shape[0]
    after = lax.broadcasted_iota(jnp.int32, (CHUNKS, LANES), 0).astype(jnp.float32) + 1.0
    for half in range(y_scr.shape[0]):
        cols = slice(half * LANES, (half + 1) * LANES)
        rate = [wide(rates, m, cols) for m in range(modes)]
        decay = [jnp.exp(-(r * float(CHUNKS))) for r in rate]
        first = tuple(wide(start, m, cols) * jnp.exp(-(rate[m] * after)) for m in range(modes))

        def step(g, terms):
            y_scr[half, pl.ds(pl.multiple_of(g * CHUNKS, CHUNKS), CHUNKS), :] = add_up(list(terms))
            return tuple(decay[m] * terms[m] for m in range(modes))

        lax.fori_loop(0, rows // CHUNKS, step, first, unroll=4)


def carry_kernel(rows_ref, before_ref, local_ref, gate_hbm, gated_ref, y_scr, gate_ref, arrived):
    fetch = pltpu.make_async_copy(gate_hbm, gate_ref, arrived)
    fetch.start()
    tokens = y_scr.shape[1]
    modes = (local_ref.shape[0] - tokens) // 2
    rates, coefs = local_ref[tokens : tokens + modes, :], local_ref[tokens + modes :, :]
    row = lax.div(lax.axis_index("context"), LOW)
    whole = jnp.exp(-(rates * float(tokens * LOW)))
    carried = jnp.zeros_like(rates)
    for q in range(rows_ref.shape[0]):
        carried = jnp.where(q < row, whole * carried + rows_ref[q].astype(jnp.float32), carried)
    start = coefs * (before_ref[...] + carried)
    from_states(rates, start, y_scr, tokens)
    fetch.wait()
    for half in range(y_scr.shape[0]):
        cols = slice(half * LANES, (half + 1) * LANES)
        gate = gate_ref[:, cols].astype(jnp.float32)
        gated_ref[:, cols] = (local_ref[:tokens, cols] + gate * y_scr[half]).astype(jnp.bfloat16)


def copy_kernel(in_ref, out_ref):
    out_ref[...] = in_ref[...]


def near_product(p0, p1, p2, p3, mine_ref, other_ref, mine_out, other_out, far_mine, far_other):
    here = lax.axis_index("tensor")
    core, y, z_hi = lax.rem(here, CORES), lax.rem(lax.div(here, CORES), Y), lax.div(here, Y * CORES)

    def block(weight_ref, z_hi, y):
        height = weight_ref.shape[0] // (2 * Y * CORES)
        first = ((z_hi * Y + y) * CORES + core) * height
        return weight_ref[pl.ds(pl.multiple_of(first, height), height), :]

    for weight, out, far in ((mine_ref, mine_out, far_mine), (other_ref, other_out, far_other)):
        total = jnp.zeros(out.shape, jnp.float32)
        for i, piece in enumerate((p0, p1, p2, p3)):
            source = lax.rem(y + Y - AWAY[i], Y)
            total += jnp.dot(piece[...], block(weight, z_hi, source), preferred_element_type=jnp.float32)
            far[i] = block(weight, 1 - z_hi, source)
        out[...] = total


def far_product(p0, p1, p2, p3, weight_ref, start_ref, out_ref):
    total = start_ref[...]
    for i, piece in enumerate((p0, p1, p2, p3)):
        total += jnp.dot(piece[...], weight_ref[i], preferred_element_type=jnp.float32)
    out_ref[...] = total.astype(out_ref.dtype)


def full(array):
    rank = len(array.shape)
    return pl.BlockSpec(array.shape, lambda *_: (0,) * rank)


def params(mebibytes):
    return pltpu.CompilerParams(vmem_limit_bytes=mebibytes * 1024 * 1024)


def cost(args, outs, flops):
    moved = sum(a.size * a.dtype.itemsize for a in (*args, *outs))
    return pl.CostEstimate(flops=flops, bytes_accessed=moved, transcendentals=0)


def call(kernel, args, outs, scratch=(), flops=0, limit=16, fetched=(), after=()):
    count, waits = len(args) + len(fetched), len(after)

    def run(*refs):
        kernel(*refs[:count], *refs[count + waits :])

    return pl.pallas_call(
        run,
        grid=(1,),
        in_specs=[
            *[full(a) for a in args],
            *[pl.BlockSpec(memory_space=pl.ANY)] * (len(fetched) + waits),
        ],
        out_specs=[full(o) for o in outs],
        out_shape=list(outs),
        scratch_shapes=list(scratch),
        compiler_params=params(limit),
        cost_estimate=cost(args, outs, flops),
    )(*args, *fetched, *after)


def body(gate_act, key_act, value_act, decay_rate, residue, skip, out_weight):
    tokens, width = gate_act.shape
    columns = out_weight.shape[1]
    parts = lax.axis_size("context")
    decay_rate, residue, skip = decay_rate.T, residue.T, skip.reshape(1, width)
    modes = decay_rate.shape[0]
    place = lax.axis_index("context")
    here = lax.axis_index("tensor")
    f32, bf16 = jnp.float32, jnp.bfloat16

    def shape(dtype, *dims):
        return jax.ShapeDtypeStruct(dims, dtype)

    halves = width // LANES
    block = pltpu.VMEM((halves, tokens, LANES), f32)

    ends_out = (shape(bf16, LOW, 2 * modes, width), shape(f32, modes, CHUNKS, width))
    ends, states = pl.pallas_call(
        ends_kernel,
        grid=(halves,),
        in_specs=[pl.BlockSpec((rows, LANES), lambda h: (0, h)) for rows in (tokens, tokens, modes)],
        out_specs=[pl.BlockSpec((*out.shape[:2], LANES), lambda h: (0, 0, h)) for out in ends_out],
        out_shape=list(ends_out),
        scratch_shapes=[pltpu.VMEM((tokens, LANES), f32), pltpu.VMEM((modes, LANES), f32)],
        compiler_params=params(58),
        cost_estimate=cost((key_act, value_act), ends_out, 2 * tokens * width * modes),
    )(key_act, value_act, decay_rate)
    with jax.named_scope("states_along_z"):
        groups = [[x * LOW + z for z in range(LOW)] for x in range(X)]
        ends = lax.all_to_all(ends, "context", 0, 0, axis_index_groups=groups)
    (local,) = call(
        local_kernel,
        (gate_act, key_act, value_act, jnp.concatenate([decay_rate, residue, skip]), states),
        (shape(f32, tokens + 2 * modes, width),),
        (block, block),
        flops=4 * tokens * width * modes,
    )
    before, rows = call(
        row_kernel, (ends,), (shape(f32, modes, width), shape(bf16, X, modes, width)), after=(local,)
    )
    with jax.named_scope("states_along_x"):
        groups = [[x * LOW + z for x in range(X)] for z in range(LOW)]
        rows = lax.all_to_all(rows, "context", 0, 0, axis_index_groups=groups)
    (gated,) = call(
        carry_kernel,
        (rows, before, local),
        (shape(bf16, tokens, width),),
        (block, pltpu.VMEM((tokens, width), bf16), pltpu.SemaphoreType.DMA),
        flops=2 * tokens * width * modes,
        fetched=(gate_act,),
    )
    with jax.named_scope("along_z"):
        far = move(gated, dz=Z // 2)
    with jax.named_scope("own_along_y"):
        *near, other_weight = lax.cond(
            place < parts,
            lambda own, weight: (*[move(own, dy=d) for d in AWAY[1:]], move(weight, dcore=1)),
            lambda own, weight: (own, own, own, weight),
            gated,
            out_weight,
        )
        near = [gated, *near]

    sums = shape(f32, tokens, columns)
    work = 2 * tokens * Y * width * columns
    picked = shape(bf16, Y, width, columns)
    mine_sum, other_sum, far_mine, far_other = call(
        near_product,
        (*near, out_weight, other_weight),
        (sums, sums, picked, picked),
        flops=2 * work,
    )
    with jax.named_scope("far_along_y"):
        (far,) = call(copy_kernel, (far,), (shape(bf16, tokens, width),), after=near[1:2])
        far = [far] + [move(far, dy=d) for d in AWAY[1:]]
    (other_sum,) = call(far_product, (*far, far_other, other_sum), (shape(bf16, tokens, columns),), flops=work)
    with jax.named_scope("sum_swap"):
        from_other = move(other_sum, dcore=1)
    (mine_sum,) = call(far_product, (*far, far_mine, mine_sum), (sums,), flops=work)
    return (mine_sum + from_other.astype(f32)).astype(bf16)


def solution(mesh):
    in_specs = (
        P("context", "tensor"),
        P("context", "tensor"),
        P("context", "tensor"),
        P("tensor", None),
        P("tensor", None),
        P("tensor"),
        P(None, "tensor"),
    )
    return jax.shard_map(body, mesh=mesh, in_specs=in_specs, out_specs=P("context", "tensor"), check_vma=False)
```

```python
import jax
import jax.numpy as jnp
from jax import lax
from jax.experimental import pallas as pl
from jax.experimental.pallas import tpu as pltpu
from jax.sharding import PartitionSpec as P

CHUNKS = 8
LANES = 128
Z, Y, CORES, X = 16, 4, 2, 4
LOW = Z // 2
AWAY = (0, -1, 1, 2)
AXES = ("tensor", "context")


def linear(x, y, z, core):
    x, y, z, core = x % X, y % Y, z % Z, core % CORES
    tensor = (z // LOW * Y + y) * CORES + core
    return tensor * (X * LOW) + x * LOW + z % LOW


def move(array, dy=0, dz=0, dcore=0):
    pairs = []
    for x in range(X):
        for y in range(Y):
            for z in range(Z):
                for core in range(CORES):
                    pairs.append((linear(x, y, z, core), linear(x, y + dy, z + dz, core + dcore)))
    return lax.ppermute(array, AXES, pairs)


def mixed_of(key_ref, value_ref):
    product = key_ref[...].astype(jnp.float32) * value_ref[...].astype(jnp.float32)
    return product.astype(jnp.bfloat16).astype(jnp.float32)


def shifted(values, by):
    rows = lax.broadcasted_iota(jnp.int32, values.shape, 0)
    return jnp.where(rows >= by, pltpu.roll(values, by, 0), 0.0)


def ends_kernel(key_ref, value_ref, decay_ref, ends_ref, states_ref, x_scr, e_scr):
    x_scr[...] = mixed_of(key_ref, value_ref)
    length = x_scr.shape[0] // CHUNKS
    modes = decay_ref.shape[0]
    rate = [jnp.broadcast_to(decay_ref[m : m + 1, :], (CHUNKS, LANES)) for m in range(modes)]
    decay = [jnp.exp(-r) for r in rate]

    def step(t, states):
        x = x_scr[pl.ds(t, CHUNKS, stride=length), :]
        return tuple(decay[m] * states[m] + x for m in range(modes))

    zero = jnp.zeros((CHUNKS, LANES), jnp.float32)
    states = lax.fori_loop(0, length, step, (zero,) * modes, unroll=4)
    later = (CHUNKS - 1 - lax.broadcasted_iota(jnp.int32, (CHUNKS, LANES), 0)).astype(jnp.float32) * float(length)
    for m in range(modes):
        states_ref[m] = states[m]
        e_scr[m : m + 1, :] = jnp.sum(jnp.exp(-(rate[m] * later)) * states[m], axis=0, keepdims=True)
    spot = lax.rem(lax.axis_index("context"), LOW)
    end, rates = e_scr[...], decay_ref[...]
    for q in range(ends_ref.shape[0]):
        to_row = jnp.maximum(q - 1 - spot, 0).astype(jnp.float32) * float(x_scr.shape[0])
        to_next = (q + ends_ref.shape[0] - 1 - spot).astype(jnp.float32) * float(x_scr.shape[0])
        ends_ref[q, :modes, :] = jnp.where(spot < q, jnp.exp(-(rates * to_row)) * end, 0.0).astype(jnp.bfloat16)
        ends_ref[q, modes:, :] = (jnp.exp(-(rates * to_next)) * end).astype(jnp.bfloat16)


def row_kernel(ends_ref, before_ref, row_ref):
    modes = before_ref.shape[0]
    total = ends_ref[0].astype(jnp.float32)
    for q in range(1, ends_ref.shape[0]):
        total += ends_ref[q].astype(jnp.float32)
    before_ref[...] = total[:modes, :]
    row_ref[...] = jnp.broadcast_to(total[modes:, :].astype(jnp.bfloat16)[None], row_ref.shape)


def wide(values, m, cols):
    return jnp.broadcast_to(values[m : m + 1, cols], (CHUNKS, LANES))


def add_up(terms):
    while len(terms) > 1:
        terms = [a + b for a, b in zip(terms[::2], terms[1::2])]
    return terms[0]


def local_kernel(gate_ref, key_ref, value_ref, modal_ref, states_ref, local_ref, x_scr, y_scr):
    mixed = mixed_of(key_ref, value_ref)
    tokens = x_scr.shape[1]
    length = tokens // CHUNKS
    modes = states_ref.shape[0]
    rates = modal_ref[:modes, :]
    coefs = modal_ref[modes : 2 * modes, :] * jnp.sqrt(2.0 * rates)
    for half in range(x_scr.shape[0]):
        cols = slice(half * LANES, (half + 1) * LANES)
        x_scr[half] = mixed[:, cols]
        rate = [wide(rates, m, cols) for m in range(modes)]
        decay = [jnp.exp(-r) for r in rate]
        coef = [wide(coefs, m, cols) for m in range(modes)]
        skip = wide(modal_ref[2 * modes : 2 * modes + 1, :], 0, cols)
        first = []
        for m in range(modes):
            total = states_ref[m, :, cols]
            by = 1
            while by < CHUNKS:
                total = total + jnp.exp(-(rate[m] * float(length * by))) * shifted(total, by)
                by *= 2
            first.append(shifted(total, 1))

        def step(t, states):
            x = x_scr[half, pl.ds(t, CHUNKS, stride=length), :]
            states = tuple(decay[m] * states[m] + x for m in range(modes))
            total = add_up([coef[m] * states[m] for m in range(modes)])
            y_scr[half, pl.ds(t, CHUNKS, stride=length), :] = total + skip * x
            return states

        lax.fori_loop(0, length, step, tuple(first), unroll=2)
        local_ref[:tokens, cols] = gate_ref[:, cols].astype(jnp.float32) * y_scr[half]
    local_ref[tokens : tokens + modes, :] = rates
    local_ref[tokens + modes :, :] = coefs


def from_states(rates, start, y_scr, rows):
    modes = rates.shape[0]
    after = lax.broadcasted_iota(jnp.int32, (CHUNKS, LANES), 0).astype(jnp.float32) + 1.0
    for half in range(y_scr.shape[0]):
        cols = slice(half * LANES, (half + 1) * LANES)
        rate = [wide(rates, m, cols) for m in range(modes)]
        decay = [jnp.exp(-(r * float(CHUNKS))) for r in rate]
        first = tuple(wide(start, m, cols) * jnp.exp(-(rate[m] * after)) for m in range(modes))

        def step(g, terms):
            y_scr[half, pl.ds(pl.multiple_of(g * CHUNKS, CHUNKS), CHUNKS), :] = add_up(list(terms))
            return tuple(decay[m] * terms[m] for m in range(modes))

        lax.fori_loop(0, rows // CHUNKS, step, first, unroll=4)


def carry_kernel(rows_ref, before_ref, local_ref, gate_hbm, gated_ref, y_scr, gate_ref, arrived):
    fetch = pltpu.make_async_copy(gate_hbm, gate_ref, arrived)
    fetch.start()
    tokens = y_scr.shape[1]
    modes = (local_ref.shape[0] - tokens) // 2
    rates, coefs = local_ref[tokens : tokens + modes, :], local_ref[tokens + modes :, :]
    row = lax.div(lax.axis_index("context"), LOW)
    whole = jnp.exp(-(rates * float(tokens * LOW)))
    carried = jnp.zeros_like(rates)
    for q in range(rows_ref.shape[0]):
        carried = jnp.where(q < row, whole * carried + rows_ref[q].astype(jnp.float32), carried)
    start = coefs * (before_ref[...] + carried)
    from_states(rates, start, y_scr, tokens)
    fetch.wait()
    for half in range(y_scr.shape[0]):
        cols = slice(half * LANES, (half + 1) * LANES)
        gate = gate_ref[:, cols].astype(jnp.float32)
        gated_ref[:, cols] = (local_ref[:tokens, cols] + gate * y_scr[half]).astype(jnp.bfloat16)


def copy_kernel(in_ref, out_ref):
    out_ref[...] = in_ref[...]


def near_product(p0, p1, p2, p3, mine_ref, other_ref, mine_out, other_out, far_mine, far_other):
    here = lax.axis_index("tensor")
    core, y, z_hi = lax.rem(here, CORES), lax.rem(lax.div(here, CORES), Y), lax.div(here, Y * CORES)

    def block(weight_ref, z_hi, y):
        height = p0.shape[1]
        cores = weight_ref.shape[0] // (2 * Y * height)
        first = ((z_hi * Y + y) * cores + core * (cores - 1)) * height
        return weight_ref[pl.ds(pl.multiple_of(first, height), height), :]

    for weight, out, far in ((mine_ref, mine_out, far_mine), (other_ref, other_out, far_other)):
        total = jnp.zeros(out.shape, jnp.float32)
        for i, piece in enumerate((p0, p1, p2, p3)):
            source = lax.rem(y + Y - AWAY[i], Y)
            total += jnp.dot(piece[...], block(weight, z_hi, source), preferred_element_type=jnp.float32)
            far[i] = block(weight, 1 - z_hi, source)
        out[...] = total


def far_product(p0, p1, p2, p3, weight_ref, start_ref, out_ref):
    total = start_ref[...]
    for i, piece in enumerate((p0, p1, p2, p3)):
        total += jnp.dot(piece[...], weight_ref[i], preferred_element_type=jnp.float32)
    out_ref[...] = total.astype(out_ref.dtype)


def full(array):
    rank = len(array.shape)
    return pl.BlockSpec(array.shape, lambda *_: (0,) * rank)


def params(mebibytes):
    return pltpu.CompilerParams(vmem_limit_bytes=mebibytes * 1024 * 1024)


def cost(args, outs, flops):
    moved = sum(a.size * a.dtype.itemsize for a in (*args, *outs))
    return pl.CostEstimate(flops=flops, bytes_accessed=moved, transcendentals=0)


def call(kernel, args, outs, scratch=(), flops=0, limit=16, fetched=(), after=()):
    count, waits = len(args) + len(fetched), len(after)

    def run(*refs):
        kernel(*refs[:count], *refs[count + waits :])

    return pl.pallas_call(
        run,
        grid=(1,),
        in_specs=[
            *[full(a) for a in args],
            *[pl.BlockSpec(memory_space=pl.ANY)] * (len(fetched) + waits),
        ],
        out_specs=[full(o) for o in outs],
        out_shape=list(outs),
        scratch_shapes=list(scratch),
        compiler_params=params(limit),
        cost_estimate=cost(args, outs, flops),
    )(*args, *fetched, *after)


def body(gate_act, key_act, value_act, decay_rate, residue, skip, out_weight):
    tokens, width = gate_act.shape
    columns = out_weight.shape[1]
    parts = lax.axis_size("context")
    decay_rate, residue, skip = decay_rate.T, residue.T, skip.reshape(1, width)
    modes = decay_rate.shape[0]
    place = lax.axis_index("context")
    here = lax.axis_index("tensor")
    f32, bf16 = jnp.float32, jnp.bfloat16

    def shape(dtype, *dims):
        return jax.ShapeDtypeStruct(dims, dtype)

    halves = width // LANES
    block = pltpu.VMEM((halves, tokens, LANES), f32)

    ends_out = (shape(bf16, LOW, 2 * modes, width), shape(f32, modes, CHUNKS, width))
    ends, states = pl.pallas_call(
        ends_kernel,
        grid=(halves,),
        in_specs=[pl.BlockSpec((rows, LANES), lambda h: (0, h)) for rows in (tokens, tokens, modes)],
        out_specs=[pl.BlockSpec((*out.shape[:2], LANES), lambda h: (0, 0, h)) for out in ends_out],
        out_shape=list(ends_out),
        scratch_shapes=[pltpu.VMEM((tokens, LANES), f32), pltpu.VMEM((modes, LANES), f32)],
        compiler_params=params(58),
        cost_estimate=cost((key_act, value_act), ends_out, 2 * tokens * width * modes),
    )(key_act, value_act, decay_rate)
    with jax.named_scope("states_along_z"):
        groups = [[x * LOW + z for z in range(LOW)] for x in range(X)]
        ends = lax.all_to_all(ends, "context", 0, 0, axis_index_groups=groups)
    (local,) = call(
        local_kernel,
        (gate_act, key_act, value_act, jnp.concatenate([decay_rate, residue, skip]), states),
        (shape(f32, tokens + 2 * modes, width),),
        (block, block),
        flops=4 * tokens * width * modes,
    )
    before, rows = call(
        row_kernel, (ends,), (shape(f32, modes, width), shape(bf16, X, modes, width)), after=(local,)
    )
    with jax.named_scope("states_along_x"):
        groups = [[x * LOW + z for x in range(X)] for z in range(LOW)]
        rows = lax.all_to_all(rows, "context", 0, 0, axis_index_groups=groups)
    (gated,) = call(
        carry_kernel,
        (rows, before, local),
        (shape(bf16, tokens, width),),
        (block, pltpu.VMEM((tokens, width), bf16), pltpu.SemaphoreType.DMA),
        flops=2 * tokens * width * modes,
        fetched=(gate_act,),
    )
    with jax.named_scope("along_z"):
        far = move(gated, dz=Z // 2)
    with jax.named_scope("own_along_y"):
        def theirs(weight):
            by_core = weight.reshape(2 * Y, CORES, width, columns)
            other = 1 - lax.rem(lax.axis_index("tensor"), CORES)
            return lax.dynamic_index_in_dim(by_core, other, 1, keepdims=False).reshape(-1, columns)

        (own,) = call(copy_kernel, (gated,), (shape(bf16, tokens, width),))
        near = [own] + [move(own, dy=d) for d in AWAY[1:]]
    with jax.named_scope("weight_swap"):
        other_weight = lax.cond(place < parts, lambda weight: move(theirs(weight), dcore=1), theirs, out_weight)

    sums = shape(f32, tokens, columns)
    work = 2 * tokens * Y * width * columns
    picked = shape(bf16, Y, width, columns)
    mine_sum, other_sum, far_mine, far_other = call(
        near_product,
        (*near, out_weight, other_weight),
        (sums, sums, picked, picked),
        flops=2 * work,
    )
    with jax.named_scope("far_along_y"):
        (far,) = call(copy_kernel, (far,), (shape(bf16, tokens, width),), after=(other_weight,))
        far = [far] + [move(far, dy=d) for d in AWAY[1:]]
    (other_sum,) = call(far_product, (*far, far_other, other_sum), (shape(bf16, tokens, columns),), flops=work)
    with jax.named_scope("sum_swap"):
        from_other = move(other_sum, dcore=1)
    (mine_sum,) = call(far_product, (*far, far_mine, mine_sum), (sums,), flops=work)
    return (mine_sum + from_other.astype(f32)).astype(bf16)


def solution(mesh):
    in_specs = (
        P("context", "tensor"),
        P("context", "tensor"),
        P("context", "tensor"),
        P("tensor", None),
        P("tensor", None),
        P("tensor"),
        P(None, "tensor"),
    )
    return jax.shard_map(body, mesh=mesh, in_specs=in_specs, out_specs=P("context", "tensor"), check_vma=False)
```

```python
import jax
import jax.numpy as jnp
from jax import lax
from jax.experimental import pallas as pl
from jax.experimental.pallas import tpu as pltpu
from jax.sharding import PartitionSpec as P

CHUNKS = 8
LANES = 128
Z, Y, CORES, X = 16, 4, 2, 4
LOW = Z // 2
AWAY = (0, -1, 1, 2)
AXES = ("tensor", "context")


def linear(x, y, z, core):
    x, y, z, core = x % X, y % Y, z % Z, core % CORES
    tensor = (z // LOW * Y + y) * CORES + core
    return tensor * (X * LOW) + x * LOW + z % LOW


def move(array, dy=0, dz=0, dcore=0):
    pairs = []
    for x in range(X):
        for y in range(Y):
            for z in range(Z):
                for core in range(CORES):
                    pairs.append((linear(x, y, z, core), linear(x, y + dy, z + dz, core + dcore)))
    return lax.ppermute(array, AXES, pairs)


def mixed_of(key_ref, value_ref):
    product = key_ref[...].astype(jnp.float32) * value_ref[...].astype(jnp.float32)
    return product.astype(jnp.bfloat16).astype(jnp.float32)


def shifted(values, by):
    rows = lax.broadcasted_iota(jnp.int32, values.shape, 0)
    return jnp.where(rows >= by, pltpu.roll(values, by, 0), 0.0)


def ends_kernel(key_ref, value_ref, decay_ref, ends_ref, states_ref, x_scr, e_scr):
    x_scr[...] = mixed_of(key_ref, value_ref)
    length = x_scr.shape[0] // CHUNKS
    modes = decay_ref.shape[0]
    rate = [jnp.broadcast_to(decay_ref[m : m + 1, :], (CHUNKS, LANES)) for m in range(modes)]
    decay = [jnp.exp(-r) for r in rate]

    def step(t, states):
        x = x_scr[pl.ds(t, CHUNKS, stride=length), :]
        return tuple(decay[m] * states[m] + x for m in range(modes))

    zero = jnp.zeros((CHUNKS, LANES), jnp.float32)
    states = lax.fori_loop(0, length, step, (zero,) * modes, unroll=16)
    later = (CHUNKS - 1 - lax.broadcasted_iota(jnp.int32, (CHUNKS, LANES), 0)).astype(jnp.float32) * float(length)
    for m in range(modes):
        states_ref[m] = states[m]
        e_scr[m : m + 1, :] = jnp.sum(jnp.exp(-(rate[m] * later)) * states[m], axis=0, keepdims=True)
    spot = lax.rem(lax.axis_index("context"), LOW)
    end, rates = e_scr[...], decay_ref[...]
    for q in range(ends_ref.shape[0]):
        to_row = jnp.maximum(q - 1 - spot, 0).astype(jnp.float32) * float(x_scr.shape[0])
        to_next = (q + ends_ref.shape[0] - 1 - spot).astype(jnp.float32) * float(x_scr.shape[0])
        ends_ref[q, :modes, :] = jnp.where(spot < q, jnp.exp(-(rates * to_row)) * end, 0.0).astype(jnp.bfloat16)
        ends_ref[q, modes:, :] = (jnp.exp(-(rates * to_next)) * end).astype(jnp.bfloat16)


def row_kernel(ends_ref, before_ref, row_ref):
    modes = before_ref.shape[0]
    total = ends_ref[0].astype(jnp.float32)
    for q in range(1, ends_ref.shape[0]):
        total += ends_ref[q].astype(jnp.float32)
    before_ref[...] = total[:modes, :]
    row_ref[...] = jnp.broadcast_to(total[modes:, :].astype(jnp.bfloat16)[None], row_ref.shape)


def wide(values, m, cols):
    return jnp.broadcast_to(values[m : m + 1, cols], (CHUNKS, LANES))


def add_up(terms):
    while len(terms) > 1:
        terms = [a + b for a, b in zip(terms[::2], terms[1::2])]
    return terms[0]


def local_kernel(gate_ref, key_ref, value_ref, modal_ref, states_ref, local_ref, x_scr, y_scr):
    mixed = mixed_of(key_ref, value_ref)
    tokens = x_scr.shape[1]
    length = tokens // CHUNKS
    modes = states_ref.shape[0]
    rates = modal_ref[:modes, :]
    coefs = modal_ref[modes : 2 * modes, :] * jnp.sqrt(2.0 * rates)
    for half in range(x_scr.shape[0]):
        cols = slice(half * LANES, (half + 1) * LANES)
        x_scr[half] = mixed[:, cols]
        rate = [wide(rates, m, cols) for m in range(modes)]
        decay = [jnp.exp(-r) for r in rate]
        coef = [wide(coefs, m, cols) for m in range(modes)]
        skip = wide(modal_ref[2 * modes : 2 * modes + 1, :], 0, cols)
        first = []
        for m in range(modes):
            total = states_ref[m, :, cols]
            by = 1
            while by < CHUNKS:
                total = total + jnp.exp(-(rate[m] * float(length * by))) * shifted(total, by)
                by *= 2
            first.append(shifted(total, 1))

        def step(t, states):
            x = x_scr[half, pl.ds(t, CHUNKS, stride=length), :]
            states = tuple(decay[m] * states[m] + x for m in range(modes))
            total = add_up([coef[m] * states[m] for m in range(modes)])
            y_scr[half, pl.ds(t, CHUNKS, stride=length), :] = total + skip * x
            return states

        lax.fori_loop(0, length, step, tuple(first), unroll=2)
        local_ref[:tokens, cols] = gate_ref[:, cols].astype(jnp.float32) * y_scr[half]
    local_ref[tokens : tokens + modes, :] = rates
    local_ref[tokens + modes :, :] = coefs


def from_states(rates, start, y_scr, rows):
    modes = rates.shape[0]
    after = lax.broadcasted_iota(jnp.int32, (CHUNKS, LANES), 0).astype(jnp.float32) + 1.0
    for half in range(y_scr.shape[0]):
        cols = slice(half * LANES, (half + 1) * LANES)
        rate = [wide(rates, m, cols) for m in range(modes)]
        decay = [jnp.exp(-(r * float(CHUNKS))) for r in rate]
        first = tuple(wide(start, m, cols) * jnp.exp(-(rate[m] * after)) for m in range(modes))

        def step(g, terms):
            y_scr[half, pl.ds(pl.multiple_of(g * CHUNKS, CHUNKS), CHUNKS), :] = add_up(list(terms))
            return tuple(decay[m] * terms[m] for m in range(modes))

        lax.fori_loop(0, rows // CHUNKS, step, first, unroll=16)


def carry_kernel(rows_ref, before_ref, local_ref, gate_hbm, gated_ref, y_scr, gate_ref, arrived):
    fetch = pltpu.make_async_copy(gate_hbm, gate_ref, arrived)
    fetch.start()
    tokens = y_scr.shape[1]
    modes = (local_ref.shape[0] - tokens) // 2
    rates, coefs = local_ref[tokens : tokens + modes, :], local_ref[tokens + modes :, :]
    row = lax.div(lax.axis_index("context"), LOW)
    whole = jnp.exp(-(rates * float(tokens * LOW)))
    carried = jnp.zeros_like(rates)
    for q in range(rows_ref.shape[0]):
        carried = jnp.where(q < row, whole * carried + rows_ref[q].astype(jnp.float32), carried)
    start = coefs * (before_ref[...] + carried)
    from_states(rates, start, y_scr, tokens)
    fetch.wait()
    for half in range(y_scr.shape[0]):
        cols = slice(half * LANES, (half + 1) * LANES)
        gate = gate_ref[:, cols].astype(jnp.float32)
        gated_ref[:, cols] = (local_ref[:tokens, cols] + gate * y_scr[half]).astype(jnp.bfloat16)


def copy_kernel(in_ref, out_ref):
    out_ref[...] = in_ref[...]


def near_product(p0, p1, p2, p3, mine_ref, other_ref, mine_out, other_out, far_mine, far_other):
    here = lax.axis_index("tensor")
    core, y, z_hi = lax.rem(here, CORES), lax.rem(lax.div(here, CORES), Y), lax.div(here, Y * CORES)

    def block(weight_ref, z_hi, y):
        height = p0.shape[1]
        cores = weight_ref.shape[0] // (2 * Y * height)
        first = ((z_hi * Y + y) * cores + core * (cores - 1)) * height
        return weight_ref[pl.ds(pl.multiple_of(first, height), height), :]

    for weight, out, far in ((mine_ref, mine_out, far_mine), (other_ref, other_out, far_other)):
        total = jnp.zeros(out.shape, jnp.float32)
        for i, piece in enumerate((p0, p1, p2, p3)):
            source = lax.rem(y + Y - AWAY[i], Y)
            total += jnp.dot(piece[...], block(weight, z_hi, source), preferred_element_type=jnp.float32)
            far[i] = block(weight, 1 - z_hi, source)
        out[...] = total


def far_product(p0, p1, p2, p3, weight_ref, start_ref, out_ref):
    total = start_ref[...]
    for i, piece in enumerate((p0, p1, p2, p3)):
        total += jnp.dot(piece[...], weight_ref[i], preferred_element_type=jnp.float32)
    out_ref[...] = total.astype(out_ref.dtype)


def full(array):
    rank = len(array.shape)
    return pl.BlockSpec(array.shape, lambda *_: (0,) * rank)


def params(mebibytes):
    return pltpu.CompilerParams(vmem_limit_bytes=mebibytes * 1024 * 1024)


def cost(args, outs, flops):
    moved = sum(a.size * a.dtype.itemsize for a in (*args, *outs))
    return pl.CostEstimate(flops=flops, bytes_accessed=moved, transcendentals=0)


def call(kernel, args, outs, scratch=(), flops=0, limit=16, fetched=(), after=()):
    count, waits = len(args) + len(fetched), len(after)

    def run(*refs):
        kernel(*refs[:count], *refs[count + waits :])

    return pl.pallas_call(
        run,
        grid=(1,),
        in_specs=[
            *[full(a) for a in args],
            *[pl.BlockSpec(memory_space=pl.ANY)] * (len(fetched) + waits),
        ],
        out_specs=[full(o) for o in outs],
        out_shape=list(outs),
        scratch_shapes=list(scratch),
        compiler_params=params(limit),
        cost_estimate=cost(args, outs, flops),
    )(*args, *fetched, *after)


def body(gate_act, key_act, value_act, decay_rate, residue, skip, out_weight):
    tokens, width = gate_act.shape
    columns = out_weight.shape[1]
    parts = lax.axis_size("context")
    decay_rate, residue, skip = decay_rate.T, residue.T, skip.reshape(1, width)
    modes = decay_rate.shape[0]
    place = lax.axis_index("context")
    here = lax.axis_index("tensor")
    f32, bf16 = jnp.float32, jnp.bfloat16

    def shape(dtype, *dims):
        return jax.ShapeDtypeStruct(dims, dtype)

    halves = width // LANES
    block = pltpu.VMEM((halves, tokens, LANES), f32)

    ends_out = (shape(bf16, LOW, 2 * modes, width), shape(f32, modes, CHUNKS, width))
    ends, states = pl.pallas_call(
        ends_kernel,
        grid=(halves,),
        in_specs=[pl.BlockSpec((rows, LANES), lambda h: (0, h)) for rows in (tokens, tokens, modes)],
        out_specs=[pl.BlockSpec((*out.shape[:2], LANES), lambda h: (0, 0, h)) for out in ends_out],
        out_shape=list(ends_out),
        scratch_shapes=[pltpu.VMEM((tokens, LANES), f32), pltpu.VMEM((modes, LANES), f32)],
        compiler_params=params(58),
        cost_estimate=cost((key_act, value_act), ends_out, 2 * tokens * width * modes),
    )(key_act, value_act, decay_rate)
    with jax.named_scope("states_along_z"):
        groups = [[x * LOW + z for z in range(LOW)] for x in range(X)]
        ends = lax.all_to_all(ends, "context", 0, 0, axis_index_groups=groups)
    (local,) = call(
        local_kernel,
        (gate_act, key_act, value_act, jnp.concatenate([decay_rate, residue, skip]), states),
        (shape(f32, tokens + 2 * modes, width),),
        (block, block),
        flops=4 * tokens * width * modes,
    )
    before, rows = call(
        row_kernel, (ends,), (shape(f32, modes, width), shape(bf16, X, modes, width)), after=(local,)
    )
    with jax.named_scope("states_along_x"):
        groups = [[x * LOW + z for x in range(X)] for z in range(LOW)]
        rows = lax.all_to_all(rows, "context", 0, 0, axis_index_groups=groups)
    (gated,) = call(
        carry_kernel,
        (rows, before, local),
        (shape(bf16, tokens, width),),
        (block, pltpu.VMEM((tokens, width), bf16), pltpu.SemaphoreType.DMA),
        flops=2 * tokens * width * modes,
        fetched=(gate_act,),
    )
    with jax.named_scope("along_z"):
        far = move(gated, dz=Z // 2)
    with jax.named_scope("own_along_y"):
        def theirs(weight):
            by_core = weight.reshape(2 * Y, CORES, width, columns)
            other = 1 - lax.rem(lax.axis_index("tensor"), CORES)
            return lax.dynamic_index_in_dim(by_core, other, 1, keepdims=False).reshape(-1, columns)

        (own,) = call(copy_kernel, (gated,), (shape(bf16, tokens, width),))
        near = [own] + [move(own, dy=d) for d in AWAY[1:]]
    with jax.named_scope("weight_swap"):
        other_weight = lax.cond(place < parts, lambda weight: move(theirs(weight), dcore=1), theirs, out_weight)

    sums = shape(f32, tokens, columns)
    work = 2 * tokens * Y * width * columns
    picked = shape(bf16, Y, width, columns)
    mine_sum, other_sum, far_mine, far_other = call(
        near_product,
        (*near, out_weight, other_weight),
        (sums, sums, picked, picked),
        flops=2 * work,
    )
    with jax.named_scope("far_along_y"):
        (far,) = call(copy_kernel, (far,), (shape(bf16, tokens, width),), after=(other_weight,))
        far = [far] + [move(far, dy=d) for d in AWAY[1:]]
    (other_sum,) = call(far_product, (*far, far_other, other_sum), (shape(bf16, tokens, columns),), flops=work)
    with jax.named_scope("sum_swap"):
        from_other = move(other_sum, dcore=1)
    (mine_sum,) = call(far_product, (*far, far_mine, mine_sum), (sums,), flops=work)
    return (mine_sum + from_other.astype(f32)).astype(bf16)


def solution(mesh):
    in_specs = (
        P("context", "tensor"),
        P("context", "tensor"),
        P("context", "tensor"),
        P("tensor", None),
        P("tensor", None),
        P("tensor"),
        P(None, "tensor"),
    )
    return jax.shard_map(body, mesh=mesh, in_specs=in_specs, out_specs=P("context", "tensor"), check_vma=False)
```

```python
import jax
import jax.numpy as jnp
from jax import lax
from jax.experimental import pallas as pl
from jax.experimental.pallas import tpu as pltpu
from jax.sharding import PartitionSpec as P

CHUNKS = 8
LANES = 128
Z, Y, CORES, X = 16, 4, 2, 4
LOW = Z // 2
AWAY = (0, -1, 1, 2)
AXES = ("tensor", "context")


def linear(x, y, z, core):
    x, y, z, core = x % X, y % Y, z % Z, core % CORES
    tensor = (z // LOW * Y + y) * CORES + core
    return tensor * (X * LOW) + x * LOW + z % LOW


def move(array, dy=0, dz=0, dcore=0):
    pairs = []
    for x in range(X):
        for y in range(Y):
            for z in range(Z):
                for core in range(CORES):
                    pairs.append((linear(x, y, z, core), linear(x, y + dy, z + dz, core + dcore)))
    return lax.ppermute(array, AXES, pairs)


def mixed_of(key_ref, value_ref):
    product = key_ref[...].astype(jnp.float32) * value_ref[...].astype(jnp.float32)
    return product.astype(jnp.bfloat16).astype(jnp.float32)


def shifted(values, by):
    rows = lax.broadcasted_iota(jnp.int32, values.shape, 0)
    return jnp.where(rows >= by, pltpu.roll(values, by, 0), 0.0)


def ends_kernel(key_ref, value_ref, decay_ref, ends_ref, states_ref, x_scr, e_scr):
    x_scr[...] = mixed_of(key_ref, value_ref)
    length = x_scr.shape[0] // CHUNKS
    modes = decay_ref.shape[0]
    rate = [jnp.broadcast_to(decay_ref[m : m + 1, :], (CHUNKS, LANES)) for m in range(modes)]
    decay = [jnp.exp(-r) for r in rate]

    def step(t, states):
        x = x_scr[pl.ds(t, CHUNKS, stride=length), :]
        return tuple(decay[m] * states[m] + x for m in range(modes))

    zero = jnp.zeros((CHUNKS, LANES), jnp.float32)
    states = lax.fori_loop(0, length, step, (zero,) * modes, unroll=16)
    later = (CHUNKS - 1 - lax.broadcasted_iota(jnp.int32, (CHUNKS, LANES), 0)).astype(jnp.float32) * float(length)
    for m in range(modes):
        states_ref[m] = states[m]
        e_scr[m : m + 1, :] = jnp.sum(jnp.exp(-(rate[m] * later)) * states[m], axis=0, keepdims=True)
    spot = lax.rem(lax.axis_index("context"), LOW)
    end, rates = e_scr[...], decay_ref[...]
    for q in range(ends_ref.shape[0]):
        to_row = jnp.maximum(q - 1 - spot, 0).astype(jnp.float32) * float(x_scr.shape[0])
        to_next = (q + ends_ref.shape[0] - 1 - spot).astype(jnp.float32) * float(x_scr.shape[0])
        ends_ref[q, :modes, :] = jnp.where(spot < q, jnp.exp(-(rates * to_row)) * end, 0.0).astype(jnp.bfloat16)
        ends_ref[q, modes:, :] = (jnp.exp(-(rates * to_next)) * end).astype(jnp.bfloat16)


def row_kernel(ends_ref, before_ref, row_ref):
    modes = before_ref.shape[0]
    total = ends_ref[0].astype(jnp.float32)
    for q in range(1, ends_ref.shape[0]):
        total += ends_ref[q].astype(jnp.float32)
    before_ref[...] = total[:modes, :]
    row_ref[...] = jnp.broadcast_to(total[modes:, :].astype(jnp.bfloat16)[None], row_ref.shape)


def wide(values, m, cols):
    return jnp.broadcast_to(values[m : m + 1, cols], (CHUNKS, LANES))


def add_up(terms):
    while len(terms) > 1:
        terms = [a + b for a, b in zip(terms[::2], terms[1::2])]
    return terms[0]


def local_kernel(gate_ref, key_ref, value_ref, modal_ref, states_ref, local_ref, x_scr, y_scr):
    mixed = mixed_of(key_ref, value_ref)
    tokens = x_scr.shape[1]
    length = tokens // CHUNKS
    modes = states_ref.shape[0]
    rates = modal_ref[:modes, :]
    coefs = modal_ref[modes : 2 * modes, :] * jnp.sqrt(2.0 * rates)
    for half in range(x_scr.shape[0]):
        cols = slice(half * LANES, (half + 1) * LANES)
        x_scr[half] = mixed[:, cols]
        rate = [wide(rates, m, cols) for m in range(modes)]
        decay = [jnp.exp(-r) for r in rate]
        coef = [wide(coefs, m, cols) for m in range(modes)]
        skip = wide(modal_ref[2 * modes : 2 * modes + 1, :], 0, cols)
        first = []
        for m in range(modes):
            total = states_ref[m, :, cols]
            by = 1
            while by < CHUNKS:
                total = total + jnp.exp(-(rate[m] * float(length * by))) * shifted(total, by)
                by *= 2
            first.append(shifted(total, 1))

        def step(t, states):
            x = x_scr[half, pl.ds(t, CHUNKS, stride=length), :]
            states = tuple(decay[m] * states[m] + x for m in range(modes))
            total = add_up([coef[m] * states[m] for m in range(modes)])
            y_scr[half, pl.ds(t, CHUNKS, stride=length), :] = total + skip * x
            return states

        lax.fori_loop(0, length, step, tuple(first), unroll=2)
        local_ref[:tokens, cols] = gate_ref[:, cols].astype(jnp.float32) * y_scr[half]
    local_ref[tokens : tokens + modes, :] = rates
    local_ref[tokens + modes :, :] = coefs


def from_states(rates, start, y_scr, rows):
    modes = rates.shape[0]
    after = lax.broadcasted_iota(jnp.int32, (CHUNKS, LANES), 0).astype(jnp.float32) + 1.0
    for half in range(y_scr.shape[0]):
        cols = slice(half * LANES, (half + 1) * LANES)
        rate = [wide(rates, m, cols) for m in range(modes)]
        decay = [jnp.exp(-(r * float(CHUNKS))) for r in rate]
        first = tuple(wide(start, m, cols) * jnp.exp(-(rate[m] * after)) for m in range(modes))

        def step(g, terms):
            y_scr[half, pl.ds(pl.multiple_of(g * CHUNKS, CHUNKS), CHUNKS), :] = add_up(list(terms))
            return tuple(decay[m] * terms[m] for m in range(modes))

        lax.fori_loop(0, rows // CHUNKS, step, first, unroll=16)


def carry_kernel(rows_ref, before_ref, local_ref, gate_hbm, gated_ref, y_scr, gate_ref, arrived):
    fetch = pltpu.make_async_copy(gate_hbm, gate_ref, arrived)
    fetch.start()
    tokens = y_scr.shape[1]
    modes = (local_ref.shape[0] - tokens) // 2
    rates, coefs = local_ref[tokens : tokens + modes, :], local_ref[tokens + modes :, :]
    row = lax.div(lax.axis_index("context"), LOW)
    whole = jnp.exp(-(rates * float(tokens * LOW)))
    carried = jnp.zeros_like(rates)
    for q in range(rows_ref.shape[0]):
        carried = jnp.where(q < row, whole * carried + rows_ref[q].astype(jnp.float32), carried)
    start = coefs * (before_ref[...] + carried)
    from_states(rates, start, y_scr, tokens)
    fetch.wait()
    for half in range(y_scr.shape[0]):
        cols = slice(half * LANES, (half + 1) * LANES)
        gate = gate_ref[:, cols].astype(jnp.float32)
        gated_ref[:, cols] = (local_ref[:tokens, cols] + gate * y_scr[half]).astype(jnp.bfloat16)


def copy_kernel(in_ref, out_ref):
    out_ref[...] = in_ref[...]


def near_product(p0, p1, p2, p3, own_far, mine_ref, other_ref, mine_out, other_out, far_mine, far_other):
    here = lax.axis_index("tensor")
    core, y, z_hi = lax.rem(here, CORES), lax.rem(lax.div(here, CORES), Y), lax.div(here, Y * CORES)

    def block(weight_ref, z_hi, y):
        height = p0.shape[1]
        cores = weight_ref.shape[0] // (2 * Y * height)
        first = ((z_hi * Y + y) * cores + core * (cores - 1)) * height
        return weight_ref[pl.ds(pl.multiple_of(first, height), height), :]

    for weight, out, far in ((mine_ref, mine_out, far_mine), (other_ref, other_out, far_other)):
        total = jnp.zeros(out.shape, jnp.float32)
        for i, piece in enumerate((p0, p1, p2, p3)):
            source = lax.rem(y + Y - AWAY[i], Y)
            total += jnp.dot(piece[...], block(weight, z_hi, source), preferred_element_type=jnp.float32)
            far[i] = block(weight, 1 - z_hi, source)
        total += jnp.dot(own_far[...], far[0], preferred_element_type=jnp.float32)
        out[...] = total


def far_product(p1, p2, p3, weight_ref, start_ref, out_ref):
    total = start_ref[...]
    for i, piece in enumerate((p1, p2, p3), 1):
        total += jnp.dot(piece[...], weight_ref[i], preferred_element_type=jnp.float32)
    out_ref[...] = total.astype(out_ref.dtype)


def full(array):
    rank = len(array.shape)
    return pl.BlockSpec(array.shape, lambda *_: (0,) * rank)


def params(mebibytes):
    return pltpu.CompilerParams(vmem_limit_bytes=mebibytes * 1024 * 1024)


def cost(args, outs, flops):
    moved = sum(a.size * a.dtype.itemsize for a in (*args, *outs))
    return pl.CostEstimate(flops=flops, bytes_accessed=moved, transcendentals=0)


def call(kernel, args, outs, scratch=(), flops=0, limit=16, fetched=(), after=()):
    count, waits = len(args) + len(fetched), len(after)

    def run(*refs):
        kernel(*refs[:count], *refs[count + waits :])

    return pl.pallas_call(
        run,
        grid=(1,),
        in_specs=[
            *[full(a) for a in args],
            *[pl.BlockSpec(memory_space=pl.ANY)] * (len(fetched) + waits),
        ],
        out_specs=[full(o) for o in outs],
        out_shape=list(outs),
        scratch_shapes=list(scratch),
        compiler_params=params(limit),
        cost_estimate=cost(args, outs, flops),
    )(*args, *fetched, *after)


def body(gate_act, key_act, value_act, decay_rate, residue, skip, out_weight):
    tokens, width = gate_act.shape
    columns = out_weight.shape[1]
    parts = lax.axis_size("context")
    decay_rate, residue, skip = decay_rate.T, residue.T, skip.reshape(1, width)
    modes = decay_rate.shape[0]
    place = lax.axis_index("context")
    here = lax.axis_index("tensor")
    f32, bf16 = jnp.float32, jnp.bfloat16

    def shape(dtype, *dims):
        return jax.ShapeDtypeStruct(dims, dtype)

    halves = width // LANES
    block = pltpu.VMEM((halves, tokens, LANES), f32)

    ends_out = (shape(bf16, LOW, 2 * modes, width), shape(f32, modes, CHUNKS, width))
    ends, states = pl.pallas_call(
        ends_kernel,
        grid=(halves,),
        in_specs=[pl.BlockSpec((rows, LANES), lambda h: (0, h)) for rows in (tokens, tokens, modes)],
        out_specs=[pl.BlockSpec((*out.shape[:2], LANES), lambda h: (0, 0, h)) for out in ends_out],
        out_shape=list(ends_out),
        scratch_shapes=[pltpu.VMEM((tokens, LANES), f32), pltpu.VMEM((modes, LANES), f32)],
        compiler_params=params(58),
        cost_estimate=cost((key_act, value_act), ends_out, 2 * tokens * width * modes),
    )(key_act, value_act, decay_rate)
    with jax.named_scope("states_along_z"):
        groups = [[x * LOW + z for z in range(LOW)] for x in range(X)]
        ends = lax.all_to_all(ends, "context", 0, 0, axis_index_groups=groups)
    (local,) = call(
        local_kernel,
        (gate_act, key_act, value_act, jnp.concatenate([decay_rate, residue, skip]), states),
        (shape(f32, tokens + 2 * modes, width),),
        (block, block),
        flops=4 * tokens * width * modes,
    )
    before, rows = call(
        row_kernel, (ends,), (shape(f32, modes, width), shape(bf16, X, modes, width)), after=(local,)
    )
    with jax.named_scope("states_along_x"):
        groups = [[x * LOW + z for x in range(X)] for z in range(LOW)]
        rows = lax.all_to_all(rows, "context", 0, 0, axis_index_groups=groups)
    (gated,) = call(
        carry_kernel,
        (rows, before, local),
        (shape(bf16, tokens, width),),
        (block, pltpu.VMEM((tokens, width), bf16), pltpu.SemaphoreType.DMA),
        flops=2 * tokens * width * modes,
        fetched=(gate_act,),
    )
    with jax.named_scope("along_z"):
        far = move(gated, dz=Z // 2)
    with jax.named_scope("own_along_y"):
        def theirs(weight):
            by_core = weight.reshape(2 * Y, CORES, width, columns)
            other = 1 - lax.rem(lax.axis_index("tensor"), CORES)
            return lax.dynamic_index_in_dim(by_core, other, 1, keepdims=False).reshape(-1, columns)

        (own,) = call(copy_kernel, (gated,), (shape(bf16, tokens, width),))
        near = [own] + [move(own, dy=d) for d in AWAY[1:]]
    with jax.named_scope("weight_swap"):
        other_weight = lax.cond(place < parts, lambda weight: move(theirs(weight), dcore=1), theirs, out_weight)

    sums = shape(f32, tokens, columns)
    work = 2 * tokens * Y * width * columns
    picked = shape(bf16, Y, width, columns)
    with jax.named_scope("far_along_y"):
        (far,) = call(copy_kernel, (far,), (shape(bf16, tokens, width),), after=(other_weight,))
        far = [far] + [move(far, dy=d) for d in AWAY[1:]]
    mine_sum, other_sum, far_mine, far_other = call(
        near_product,
        (*near, far[0], out_weight, other_weight),
        (sums, sums, picked, picked),
        flops=2 * work,
    )
    (other_sum,) = call(far_product, (*far[1:], far_other, other_sum), (shape(bf16, tokens, columns),), flops=work)
    with jax.named_scope("sum_swap"):
        from_other = move(other_sum, dcore=1)
    (mine_sum,) = call(far_product, (*far[1:], far_mine, mine_sum), (sums,), flops=work)
    return (mine_sum + from_other.astype(f32)).astype(bf16)


def solution(mesh):
    in_specs = (
        P("context", "tensor"),
        P("context", "tensor"),
        P("context", "tensor"),
        P("tensor", None),
        P("tensor", None),
        P("tensor"),
        P(None, "tensor"),
    )
    return jax.shard_map(body, mesh=mesh, in_specs=in_specs, out_specs=P("context", "tensor"), check_vma=False)
```
